256 devices in a mesh: dp: 16 (over z, core), tensor: 16 (over x, y).
Axes of the slice: x: 4, y: 4, z: 8, core: 2. Of those that a mesh axis runs over, the one named last changes fastest.
Arguments:
- input_acts: bfloat16 [14336, 8192], P('dp', 'tensor'), may hold values from -6 to 6
- out_grad: bfloat16 [14336, 8192], P('dp', 'tensor'), may hold values from -6 to 6
- base_weight: bfloat16 [8192, 8192], P(None, 'tensor'), may hold values from -0.0625 to 0.0625
- factor_a: bfloat16 [64, 32, 8192], P('dp', None, 'tensor'), may hold values from -6 to 6
- factor_b: bfloat16 [64, 32, 8192], P('dp', None, 'tensor'), may hold values from -6 to 6
- block_adapter: int32 [112], P('dp'), may hold values from 0 to 63, as said below
- adapter_slot: int32 [64], replicated, may hold values from 0 to 63, as said below
- rollout_map: int32 [16, 8], P('dp'), may hold values from 0 to 63
Outputs:
- input_gradient: bfloat16 [14336, 8192], P('dp', 'tensor')
- new_a: bfloat16 [64, 32, 8192], P('dp', None, 'tensor')
- new_b: bfloat16 [64, 32, 8192], P('dp', None, 'tensor')
- rollout_a: bfloat16 [128, 32, 8192], P('dp', None, 'tensor')
- rollout_b: bfloat16 [128, 32, 8192], P('dp', None, 'tensor')
The draws below stay inside these ranges and needn't reach their ends.
Inputs may be any that keep to these rules, and one draw needn't show every extreme that they name: `block_adapter`: block b covers token rows b * 128 to (b + 1) * 128 - 1. The owner of an adapter is the dp index adapter_slot[adapter] // 4. Among the 7 blocks of one dp index, at most 1 have adapters of one owner. `adapter_slot`: each slot is taken by exactly one adapter.
All inputs are finite; a program needn't handle non-finite values.
Results may differ from the reference program's by a relative error of at most 0.02.
Values may be sent and summed in bfloat16 or wider, within the bound.
No kernel may reach another device: no remote copies, remote signals or barrier semaphores. Data moves between devices by JAX's collectives and lax.ppermute only.
A program may use at most 128 MiB of HBM per device.

```python
import math
import jax
import jax.numpy as jnp
from jax import lax

INPUT_FEATURES = 8192
DOUT = 8192
ADAPTER_RANK = 32
ADAPTERS = 64
BLOCK = 128
ROLLOUT = 8
TOK_DEV = 896
TOKEN_TOTAL = 14336
N_DP = 16
N_TENSOR = 16


def layout(key):
    streams = jax.random.split(key, 6)
    slot_table = jax.random.permutation(streams[0], ADAPTERS).astype(jnp.int32)
    per_owner = ADAPTERS // N_DP
    block_count = TOK_DEV // BLOCK
    busiest = jax.random.randint(streams[1], (), 0, N_DP)
    owner_ids = jnp.arange(N_DP, dtype=jnp.int32)
    owner_score = jax.random.randint(streams[2], (N_DP, N_DP), 0, 2 ** 20) * N_DP + owner_ids[None, :]
    owner_score = jnp.where(owner_ids[None, :] == busiest, -1, owner_score)
    ranking = jnp.argsort(owner_score, axis=1, stable=True).astype(jnp.int32)[:, :block_count]
    positions = jnp.arange(block_count, dtype=jnp.int32)
    shuffle = jnp.argsort(jax.random.randint(streams[4], (N_DP, block_count), 0, 2 ** 20) * block_count + positions[None, :], axis=1, stable=True)
    owners = jnp.take_along_axis(ranking, shuffle, axis=1)
    within = jax.random.randint(streams[5], (N_DP, block_count), 0, per_owner)
    block_slots = owners * per_owner + within
    adapter_table = jnp.argsort(slot_table, stable=True).astype(jnp.int32)
    return (slot_table, adapter_table[block_slots].reshape(-1).astype(jnp.int32))


def draw_adapter_slot(key, part):
    return layout(key)[0]


def draw_block_adapter(key, part):
    return layout(key)[1]


def touch_ends(values, stream_key, low, largest):
    shape = values.shape
    place = [jax.random.randint(jax.random.fold_in(stream_key, axis), (), 0, shape[axis]) for axis in range(len(shape))]
    values = values.at[tuple(place)].set(low)
    longest = shape.index(max(shape))
    place[longest] = (place[longest] + 1) % shape[longest]
    return values.at[tuple(place)].set(largest)


def block_levels(own_key, shape, pieces, smallest, top_value):
    def one(axis_at, parts):
        draws = jax.random.uniform(jax.random.fold_in(jax.random.fold_in(own_key, 6), axis_at), (parts,), jnp.float32, smallest / len(pieces), top_value / len(pieces))
        return jnp.repeat(jnp.exp(draws), shape[axis_at] // parts).reshape((-1,) + (1,) * (len(shape) - axis_at - 1))

    loudness = one(*pieces[0])
    for cut in pieces[1:]:
        loudness = loudness * one(*cut)
    return loudness


def gaussian(stream_key, shape, scale, limit, pieces=(), held_as=jnp.bfloat16):
    drawn = scale * jax.random.normal(stream_key, shape, jnp.float32)
    if pieces:
        drawn = drawn * block_levels(stream_key, shape, pieces, -0.22, 0.18)
    return jnp.clip(drawn, -limit, limit).astype(held_as)


def setup_inputs(seed: int = 0) -> dict:
    splits = jax.random.split(jax.random.key(seed), 9)
    input_acts = gaussian(splits[0], (TOKEN_TOTAL, INPUT_FEATURES), 1.0, 6.0, ((0, 16), (1, 16)))
    out_grad = gaussian(splits[1], (TOKEN_TOTAL, DOUT), 1.0, 6.0, ((0, 16), (1, 16)))
    base_weight = gaussian(splits[2], (INPUT_FEATURES, DOUT), DOUT ** -0.5, 0.0625, ((1, 16),))
    factor_a = gaussian(splits[3], (ADAPTERS, ADAPTER_RANK, INPUT_FEATURES), 1.0, 6.0, ((0, 16), (2, 16)))
    factor_b = gaussian(splits[4], (ADAPTERS, ADAPTER_RANK, DOUT), 1.0, 6.0, ((0, 16), (2, 16)))
    block_adapter = draw_block_adapter(jax.random.fold_in(splits[8], 71), 0)
    adapter_slot = draw_adapter_slot(jax.random.fold_in(splits[8], 71), 0)
    rollout_map = touch_ends(jax.random.randint(splits[7], (N_DP, ROLLOUT), 0, ADAPTERS), jax.random.fold_in(splits[7], 1), 0, ADAPTERS - 1).astype(jnp.int32)
    return {"input_acts": input_acts, "out_grad": out_grad, "base_weight": base_weight, "factor_a": factor_a, "factor_b": factor_b, "block_adapter": block_adapter, "adapter_slot": adapter_slot, "rollout_map": rollout_map}


learn_rate = 0.25

def reference(input_acts, out_grad, base_weight, factor_a, factor_b, block_adapter, adapter_slot, rollout_map):
    adapter_scale = 1.0 / math.sqrt(INPUT_FEATURES * ADAPTER_RANK)
    shard_width = DOUT // N_TENSOR
    frozen_output = jnp.zeros((TOKEN_TOTAL, INPUT_FEATURES), jnp.float32)
    for group in range(N_TENSOR):
        partial_value = lax.dot_general(out_grad[:, group * shard_width:(group + 1) * shard_width], base_weight[:, group * shard_width:(group + 1) * shard_width], (((1,), (1,)), ((), ())), preferred_element_type=jnp.float32)
        rounded = lax.optimization_barrier(partial_value.astype(jnp.bfloat16))
        frozen_output = frozen_output + rounded.astype(jnp.float32)
    block_slots = adapter_slot[block_adapter].astype(jnp.int32)
    block_count = TOKEN_TOTAL // BLOCK
    activation_blocks = input_acts.reshape(block_count, BLOCK, INPUT_FEATURES).astype(jnp.float32)
    gradient_blocks = out_grad.reshape(block_count, BLOCK, DOUT).astype(jnp.float32)
    selected_down_factor = factor_a[block_slots].astype(jnp.float32)
    chosen_b = factor_b[block_slots].astype(jnp.float32)
    rank_projected_down = jnp.einsum('nbo,nro->nrb', gradient_blocks, chosen_b)
    rank_projected_down = lax.optimization_barrier(rank_projected_down.astype(jnp.bfloat16)).astype(jnp.float32)
    rank_projected_up = jnp.einsum('nbi,nri->nrb', activation_blocks, selected_down_factor)
    rank_projected_up = lax.optimization_barrier(rank_projected_up.astype(jnp.bfloat16)).astype(jnp.float32)
    adapter_term = jnp.einsum('scz,scl->szl', rank_projected_down, selected_down_factor).reshape(TOKEN_TOTAL, INPUT_FEATURES)
    input_gradient = (frozen_output + adapter_scale * adapter_term).astype(jnp.bfloat16)
    down_contribution = adapter_scale * jnp.einsum('tvm,tma->tva', rank_projected_down, activation_blocks)
    up_contribution = adapter_scale * jnp.einsum('vte,vez->vtz', rank_projected_up, gradient_blocks)
    grad_a = jax.ops.segment_sum(down_contribution, block_slots, num_segments=ADAPTERS)
    grad_b = jax.ops.segment_sum(up_contribution, block_slots, num_segments=ADAPTERS)
    new_a = (factor_a.astype(jnp.float32) - learn_rate * grad_a).astype(jnp.bfloat16)
    new_b = (factor_b.astype(jnp.float32) - learn_rate * grad_b).astype(jnp.bfloat16)
    rollout_slots = adapter_slot[rollout_map.reshape(-1)].astype(jnp.int32)
    return (input_gradient, new_a, new_b, new_a[rollout_slots], new_b[rollout_slots])
```

```python
import functools
import math

import jax
import jax.numpy as jnp
from jax import lax
from jax.experimental import pallas as pl
from jax.experimental.pallas import tpu as pltpu
from jax.sharding import PartitionSpec as P

INPUT_FEATURES = 8192
ADAPTER_RANK = 32
BLOCK = 128
CORES = 2
SIDE = 4
LEARN_RATE = 0.25
SCALE = 1.0 / math.sqrt(INPUT_FEATURES * ADAPTER_RANK)

BF = jnp.bfloat16
F32 = jnp.float32
SMEM = functools.partial(pl.BlockSpec, memory_space=pltpu.SMEM)
VMEM = functools.partial(pl.BlockSpec, memory_space=pltpu.VMEM)
ANY = functools.partial(pl.BlockSpec, memory_space=pl.ANY)
PARAMS = pltpu.CompilerParams(vmem_limit_bytes=32 * 2**20)


def slot_lookup(adapter_ids, adapter_slot):
    matches = adapter_ids[:, None] == jnp.arange(adapter_slot.shape[0], dtype=jnp.int32)[None, :]
    return jnp.sum(jnp.where(matches, adapter_slot[None, :], 0), axis=1)


def z_hop(x, step):
    n = lax.axis_size("dp")
    chips = n // CORES
    perm = [(d, (d // CORES + step) % chips * CORES + d % CORES) for d in range(n)]
    return lax.ppermute(x, "dp", perm)


def core_swap(x):
    n = lax.axis_size("dp")
    return lax.ppermute(x, "dp", [(d, d ^ 1) for d in range(n)])


def plane_hop(x, step, axis):
    n = lax.axis_size("tensor")
    if axis == "y":
        perm = [(t, t // SIDE * SIDE + (t + step) % SIDE) for t in range(n)]
    else:
        perm = [(t, (t + step * SIDE) % n) for t in range(n)]
    return lax.ppermute(x, "tensor", perm)


def ring_gather(x):
    half = (x.shape[0] + 1) // 2
    up = down = x
    parts = {0: [x]}
    for step in range(1, 4):
        up, down = z_hop(up, 1), z_hop(down, -1)
        parts[8 - step] = [up]
        parts[step] = [down]
    parts[4] = [z_hop(up[:half], 1), z_hop(down[half:], -1)]
    return [piece for place in range(8) for piece in parts[place]]


def fetch(sources, target, sems, first):
    copies, row = [], 0
    for k, ref in enumerate(sources):
        rows = ref.shape[0]
        copies.append(pltpu.make_async_copy(ref, target.at[pl.ds(row, rows)], sems.at[first + k]))
        row += rows
    for copy in copies:
        copy.start()
    return copies


def select_kernel(blocks, rolls, *refs):
    place, refs = refs[0], refs[1:]
    a_refs, b_refs = refs[:9], refs[9:18]
    mine_ref, other_ref, mine_roll, other_roll, hold_a, hold_b, sems = refs[18:]
    copies = fetch(a_refs, hold_a, sems, 0) + fetch(b_refs, hold_b, sems, 9)
    for copy in copies:
        copy.wait()
    need = blocks + rolls
    for n in range(blocks):
        mine_ref[n] = hold_a[place[n]]
        mine_ref[blocks + n] = hold_b[place[n]]
        other_ref[n] = hold_a[place[need + n]]
        other_ref[blocks + n] = hold_b[place[need + n]]
    for n in range(rolls):
        mine_roll[n] = hold_a[place[blocks + n]]
        mine_roll[rolls + n] = hold_b[place[blocks + n]]
        other_roll[n] = hold_a[place[need + blocks + n]]
        other_roll[rolls + n] = hold_b[place[need + blocks + n]]


def select(place, parts_a, parts_b, blocks, rolls):
    slots, rank, width = 8 * parts_a[0].shape[0], *parts_a[0].shape[1:]
    shape = lambda n: jax.ShapeDtypeStruct((n, rank, width), BF)
    return pl.pallas_call(
        functools.partial(select_kernel, blocks, rolls),
        out_shape=(shape(2 * blocks), shape(2 * blocks), shape(2 * rolls), shape(2 * rolls)),
        in_specs=[SMEM()] + [ANY()] * 18,
        out_specs=(VMEM(),) * 4,
        scratch_shapes=[
            pltpu.VMEM((slots, rank, width), BF),
            pltpu.VMEM((slots, rank, width), BF),
            pltpu.SemaphoreType.DMA((18,)),
        ],
        compiler_params=PARAMS,
        cost_estimate=pl.CostEstimate(flops=0, bytes_accessed=8 * 2**20, transcendentals=0),
        name="select_factors",
    )(place, *parts_a, *parts_b)


def project_kernel(blocks, own_ref, mine_ref, other_ref, acts_ref, grad_ref, chosen_ref, out_ref):
    for n in range(blocks):
        own = own_ref[n] == 1
        rows = pl.ds(n * BLOCK, BLOCK)
        factor_a = jnp.where(own, mine_ref[n], other_ref[n])
        factor_b = jnp.where(own, mine_ref[blocks + n], other_ref[blocks + n])
        chosen_ref[n] = factor_a
        contract = (((1,), (1,)), ((), ()))
        out_ref[n] = lax.dot_general(
            factor_b, grad_ref[rows, :], contract, preferred_element_type=F32
        ).astype(BF)
        out_ref[blocks + n] = lax.dot_general(
            factor_a, acts_ref[rows, :], contract, preferred_element_type=F32
        ).astype(BF)


def project(own, mine, other, acts, grad):
    blocks, (rank, width) = mine.shape[0] // 2, mine.shape[1:]
    return pl.pallas_call(
        functools.partial(project_kernel, blocks),
        out_shape=(
            jax.ShapeDtypeStruct((blocks, rank, width), BF),
            jax.ShapeDtypeStruct((2 * blocks, rank, BLOCK), BF),
        ),
        in_specs=[SMEM()] + [VMEM()] * 4,
        out_specs=(VMEM(),) * 2,
        compiler_params=PARAMS,
        cost_estimate=pl.CostEstimate(flops=0, bytes_accessed=8 * 2**20, transcendentals=0),
        name="project_ranks",
    )(own, mine, other, acts, grad)


def plane_sum(x):
    for axis in ("y", "x"):
        terms = [x] + [plane_hop(x, step, axis) for step in (1, 3, 2)]
        x = sum(term.astype(F32) for term in terms).astype(BF)
    return x


def contribute_kernel(blocks, ranks_ref, acts_ref, grad_ref, a_ref, b_ref):
    for n in range(blocks):
        rows = pl.ds(n * BLOCK, BLOCK)
        a_ref[n] = (
            SCALE * jnp.dot(ranks_ref[n], acts_ref[rows, :], preferred_element_type=F32)
        ).astype(BF)
        b_ref[n] = (
            SCALE * jnp.dot(ranks_ref[blocks + n], grad_ref[rows, :], preferred_element_type=F32)
        ).astype(BF)


def contribute(ranks, acts, grad):
    blocks, rank, width = ranks.shape[0] // 2, ranks.shape[1], acts.shape[1]
    shape = jax.ShapeDtypeStruct((blocks, rank, width), BF)
    return pl.pallas_call(
        functools.partial(contribute_kernel, blocks),
        out_shape=(shape, shape),
        in_specs=[VMEM()] * 3,
        out_specs=(VMEM(),) * 2,
        compiler_params=PARAMS,
        cost_estimate=pl.CostEstimate(flops=0, bytes_accessed=8 * 2**20, transcendentals=0),
        name="factor_contributions",
    )(ranks, acts, grad)


def total_kernel(needs, *refs):
    place, used, refs = refs[0], refs[1], refs[2:]
    a_refs, b_refs = refs[:9], refs[9:18]
    mine_ref, other_ref, hold_a, hold_b, sems = refs[18:]
    copies = fetch(a_refs, hold_a, sems, 0) + fetch(b_refs, hold_b, sems, 9)
    for copy in copies:
        copy.wait()

    def one(need, hold):
        def term(source):
            at = need * 8 + source
            return hold[place[at]].astype(F32) * used[at].astype(F32)

        value = term(0)
        for source in range(1, 8):
            value += term(source)
        return value

    @pl.loop(0, needs)
    def _(need):
        mine_ref[need] = one(need, hold_a)
        mine_ref[needs + need] = one(need, hold_b)
        other_ref[need] = one(needs + need, hold_a).astype(BF)
        other_ref[needs + need] = one(needs + need, hold_b).astype(BF)


def total(place, used, parts_a, parts_b, needs):
    blocks, (rank, width) = 8 * parts_a[0].shape[0], parts_a[0].shape[1:]
    return pl.pallas_call(
        functools.partial(total_kernel, needs),
        out_shape=(
            jax.ShapeDtypeStruct((2 * needs, rank, width), F32),
            jax.ShapeDtypeStruct((2 * needs, rank, width), BF),
        ),
        in_specs=[SMEM()] * 2 + [ANY()] * 18,
        out_specs=(VMEM(),) * 2,
        scratch_shapes=[
            pltpu.VMEM((blocks, rank, width), BF),
            pltpu.VMEM((blocks, rank, width), BF),
            pltpu.SemaphoreType.DMA((18,)),
        ],
        compiler_params=PARAMS,
        cost_estimate=pl.CostEstimate(flops=0, bytes_accessed=16 * 2**20, transcendentals=0),
        name="gradient_totals",
    )(place, used, *parts_a, *parts_b)


def update_kernel(
    slots, rolls, own_ref, a_ref, b_ref, mine_roll, other_roll, mine_ref, other_ref,
    new_a, new_b, roll_a, roll_b,
):
    needs = slots + rolls

    def fresh(factor, at):
        gradient = mine_ref[at] + other_ref[at].astype(F32)
        return (factor.astype(F32) - LEARN_RATE * gradient).astype(BF)

    for n in range(slots):
        new_a[n] = fresh(a_ref[n], n)
        new_b[n] = fresh(b_ref[n], needs + n)
    for n in range(rolls):
        own = own_ref[n] == 1
        roll_a[n] = fresh(jnp.where(own, mine_roll[n], other_roll[n]), slots + n)
        roll_b[n] = fresh(
            jnp.where(own, mine_roll[rolls + n], other_roll[rolls + n]), needs + slots + n
        )


def update(own, factor_a, factor_b, mine_roll, other_roll, mine, other):
    slots, rank, width = factor_a.shape
    rolls = mine_roll.shape[0] // 2
    shape = lambda n: jax.ShapeDtypeStruct((n, rank, width), BF)
    return pl.pallas_call(
        functools.partial(update_kernel, slots, rolls),
        out_shape=(shape(slots), shape(slots), shape(rolls), shape(rolls)),
        in_specs=[SMEM()] + [VMEM()] * 6,
        out_specs=(VMEM(),) * 4,
        compiler_params=PARAMS,
        cost_estimate=pl.CostEstimate(flops=0, bytes_accessed=8 * 2**20, transcendentals=0),
        name="update_factors",
    )(own, factor_a, factor_b, mine_roll, other_roll, mine, other)


def finish_kernel(blocks, ranks_ref, chosen_ref, base_ref, out_ref):
    for n in range(blocks):
        rows = pl.ds(n * BLOCK, BLOCK)
        term = lax.dot_general(
            ranks_ref[n], chosen_ref[n], (((0,), (0,)), ((), ())), preferred_element_type=F32
        )
        out_ref[rows, :] = (base_ref[rows, :].astype(F32) + SCALE * term).astype(BF)


def finish(ranks, chosen, base):
    blocks = chosen.shape[0]
    return pl.pallas_call(
        functools.partial(finish_kernel, blocks),
        out_shape=jax.ShapeDtypeStruct(base.shape, BF),
        in_specs=[VMEM()] * 3,
        out_specs=VMEM(),
        compiler_params=PARAMS,
        cost_estimate=pl.CostEstimate(flops=0, bytes_accessed=4 * 2**20, transcendentals=0),
        name="input_gradient",
    )(ranks, chosen, base)


def per_device(
    input_acts, out_grad, base_weight, factor_a, factor_b, block_adapter, adapter_slot, rollout_map
):
    blocks = block_adapter.shape[0]
    slots = factor_a.shape[0]
    rolls = rollout_map.size
    groups = lax.axis_size("dp")
    chips = groups // CORES
    me = lax.axis_index("dp")
    chip, core = me // CORES, me % CORES

    wanted = slot_lookup(jnp.concatenate([block_adapter, rollout_map.reshape(-1)]), adapter_slot)
    table = lax.all_gather(wanted, "dp", axis=0, tiled=False)
    device_ids = jnp.arange(groups, dtype=jnp.int32)

    def row_of(device):
        return jnp.sum(jnp.where(device_ids[:, None] == device, table, 0), axis=0)

    other = me ^ 1
    other_wanted = row_of(other)

    def places(slot_ids):
        owner = slot_ids // slots
        here = owner % CORES == core
        distance = (owner // CORES - chip + chips) % chips
        return jnp.where(here, distance * slots + slot_ids % slots, 0), here.astype(jnp.int32)

    mine_place, mine_own = places(wanted)
    other_place, _ = places(other_wanted)

    ring = jnp.stack([row_of((chip + k) % chips * CORES + core)[:blocks] for k in range(chips)])
    own_slots = jnp.arange(slots, dtype=jnp.int32)
    need = jnp.concatenate(
        [me * slots + own_slots, wanted[blocks:], other * slots + own_slots, other_wanted[blocks:]]
    )
    match = (need[:, None, None] == ring[None]).astype(jnp.int32)
    used = jnp.sum(match, axis=2)
    at_block = jnp.sum(match * jnp.arange(blocks, dtype=jnp.int32)[None, None], axis=2)
    source = jnp.arange(chips, dtype=jnp.int32)[None, :] * blocks + at_block
    source, used = source.reshape(-1), used.reshape(-1)

    rows = input_acts.shape[0] // 2
    sums = []
    for part in range(2):
        partial_value = lax.dot_general(
            out_grad[part * rows : (part + 1) * rows],
            base_weight,
            (((1,), (1,)), ((), ())),
            preferred_element_type=F32,
        ).astype(BF)
        sums.append(
            lax.psum_scatter(partial_value, "tensor", scatter_dimension=1, tiled=True)
        )

    parts_a, parts_b = ring_gather(factor_a), ring_gather(factor_b)
    mine_sel, other_sel, mine_roll, other_roll = select(
        jnp.concatenate([mine_place, other_place]), parts_a, parts_b, blocks, rolls
    )
    got_sel = core_swap(other_sel)
    got_roll = core_swap(other_roll)
    chosen_a, rank_parts = project(mine_own[:blocks], mine_sel, got_sel, input_acts, out_grad)
    ranks = plane_sum(rank_parts)
    part_a, part_b = contribute(ranks, input_acts, out_grad)
    mine_total, other_total = total(
        source, used, ring_gather(part_a), ring_gather(part_b), slots + rolls
    )
    got_total = core_swap(other_total)
    new_a, new_b, roll_a, roll_b = update(
        mine_own[blocks:], factor_a, factor_b, mine_roll, got_roll, mine_total, got_total
    )
    base = jnp.concatenate(sums, axis=0)
    return finish(ranks, chosen_a, base), new_a, new_b, roll_a, roll_b


def solution(mesh):
    return jax.shard_map(
        per_device,
        mesh=mesh,
        in_specs=(
            P("dp", "tensor"),
            P("dp", "tensor"),
            P(None, "tensor"),
            P("dp", None, "tensor"),
            P("dp", None, "tensor"),
            P("dp"),
            P(),
            P("dp", None),
        ),
        out_specs=(
            P("dp", "tensor"),
            P("dp", None, "tensor"),
            P("dp", None, "tensor"),
            P("dp", None, "tensor"),
            P("dp", None, "tensor"),
        ),
        check_vma=False,
    )
```

```python
import functools
import math

import jax
import jax.numpy as jnp
from jax import lax
from jax.experimental import pallas as pl
from jax.experimental.pallas import tpu as pltpu
from jax.sharding import PartitionSpec as P

INPUT_FEATURES = 8192
ADAPTER_RANK = 32
BLOCK = 128
CORES = 2
SIDE = 4
LEARN_RATE = 0.25
SCALE = 1.0 / math.sqrt(INPUT_FEATURES * ADAPTER_RANK)

BF = jnp.bfloat16
F32 = jnp.float32
SMEM = functools.partial(pl.BlockSpec, memory_space=pltpu.SMEM)
VMEM = functools.partial(pl.BlockSpec, memory_space=pltpu.VMEM)
ANY = functools.partial(pl.BlockSpec, memory_space=pl.ANY)
PARAMS = pltpu.CompilerParams(vmem_limit_bytes=32 * 2**20)


def slot_lookup(adapter_ids, adapter_slot):
    matches = adapter_ids[:, None] == jnp.arange(adapter_slot.shape[0], dtype=jnp.int32)[None, :]
    return jnp.sum(jnp.where(matches, adapter_slot[None, :], 0), axis=1)


def z_hop(x, step):
    n = lax.axis_size("dp")
    chips = n // CORES
    perm = [(d, (d // CORES + step) % chips * CORES + d % CORES) for d in range(n)]
    return lax.ppermute(x, "dp", perm)


def core_swap(x):
    n = lax.axis_size("dp")
    return lax.ppermute(x, "dp", [(d, d ^ 1) for d in range(n)])


def plane_hop(x, step, axis):
    n = lax.axis_size("tensor")
    if axis == "y":
        perm = [(t, t // SIDE * SIDE + (t + step) % SIDE) for t in range(n)]
    else:
        perm = [(t, (t + step * SIDE) % n) for t in range(n)]
    return lax.ppermute(x, "tensor", perm)


def ring_gather(p, q):
    found = []
    last = []
    for x in (p, q):
        up = down = x
        parts = {0: x}
        for step in range(1, 4):
            up, down = z_hop(up, 1), z_hop(down, -1)
            parts[8 - step], parts[step] = up, down
        found.append(parts)
        last.append((up, down))
    found[0][4] = z_hop(last[0][0], 1)
    found[1][4] = z_hop(last[1][1], -1)
    return [[parts[place] for place in range(8)] for parts in found]


def fetch(sources, target, sems, first):
    copies, row = [], 0
    for k, ref in enumerate(sources):
        rows = ref.shape[0]
        copies.append(pltpu.make_async_copy(ref, target.at[pl.ds(row, rows)], sems.at[first + k]))
        row += rows
    for copy in copies:
        copy.start()
    return copies


def select_kernel(blocks, rolls, slots, rank, *refs):
    place, refs = refs[0], refs[1:]
    a_refs, b_refs = refs[:8], refs[8:16]
    mine_ref, other_ref, mine_roll, other_roll, ids_ref, hold_a, hold_b, sems = refs[16:]
    copies = fetch(a_refs, hold_a, sems, 0) + fetch(b_refs, hold_b, sems, 8)
    for copy in copies:
        copy.wait()
    need = blocks + rolls
    tail = b_refs[0].shape[0] - slots * rank

    def from_a(at):
        return hold_a[pl.ds(pl.multiple_of(place[at] * rank, rank), rank), :]

    def from_b(at):
        row = place[at] * rank + place[at] // slots * tail
        return hold_b[pl.ds(pl.multiple_of(row, 16), rank), :]

    for n in range(blocks):
        mine_ref[n] = from_a(n)
        mine_ref[blocks + n] = from_b(n)
        other_ref[n] = from_a(need + n)
        other_ref[blocks + n] = from_b(need + n)
    for n in range(rolls):
        mine_roll[n] = from_a(blocks + n)
        mine_roll[rolls + n] = from_b(blocks + n)
        other_roll[n] = from_a(need + blocks + n)
        other_roll[rolls + n] = from_b(need + blocks + n)
    for k in range(8):
        row = k * (slots * rank + tail) + slots * rank
        ids_ref[k] = hold_b[row : row + tail, : ids_ref.shape[2]]


def select(place, parts_a, parts_b, blocks, rolls, slots):
    rows, width = parts_a[0].shape
    rank = rows // slots
    tall = parts_b[0].shape[0]
    shape = lambda n: jax.ShapeDtypeStruct((n, rank, width), BF)
    return pl.pallas_call(
        functools.partial(select_kernel, blocks, rolls, slots, rank),
        out_shape=(
            shape(2 * blocks), shape(2 * blocks), shape(2 * rolls), shape(2 * rolls),
            jax.ShapeDtypeStruct((8, tall - rows, 128), BF),
        ),
        in_specs=[SMEM()] + [ANY()] * 16,
        out_specs=(VMEM(),) * 5,
        scratch_shapes=[
            pltpu.VMEM((8 * rows, width), BF),
            pltpu.VMEM((8 * tall, width), BF),
            pltpu.SemaphoreType.DMA((16,)),
        ],
        compiler_params=PARAMS,
        cost_estimate=pl.CostEstimate(flops=0, bytes_accessed=8 * 2**20, transcendentals=0),
        name="select_factors",
    )(place, *parts_a, *parts_b)


def project_kernel(blocks, own_ref, mine_ref, other_ref, acts_ref, grad_ref, chosen_ref, out_ref):
    for n in range(blocks):
        own = own_ref[n] == 1
        rows = pl.ds(n * BLOCK, BLOCK)
        factor_a = jnp.where(own, mine_ref[n], other_ref[n])
        factor_b = jnp.where(own, mine_ref[blocks + n], other_ref[blocks + n])
        chosen_ref[n] = factor_a
        contract = (((1,), (1,)), ((), ()))
        out_ref[n] = lax.dot_general(
            factor_b, grad_ref[rows, :], contract, preferred_element_type=F32
        ).astype(BF)
        out_ref[blocks + n] = lax.dot_general(
            factor_a, acts_ref[rows, :], contract, preferred_element_type=F32
        ).astype(BF)


def project(own, mine, other, acts, grad):
    blocks, (rank, width) = mine.shape[0] // 2, mine.shape[1:]
    return pl.pallas_call(
        functools.partial(project_kernel, blocks),
        out_shape=(
            jax.ShapeDtypeStruct((blocks, rank, width), BF),
            jax.ShapeDtypeStruct((2 * blocks, rank, BLOCK), BF),
        ),
        in_specs=[SMEM()] + [VMEM()] * 4,
        out_specs=(VMEM(),) * 2,
        compiler_params=PARAMS,
        cost_estimate=pl.CostEstimate(flops=0, bytes_accessed=8 * 2**20, transcendentals=0),
        name="project_ranks",
    )(own, mine, other, acts, grad)


def plane_sum(x):
    for axis in ("y", "x"):
        terms = [x] + [plane_hop(x, step, axis) for step in (1, 3, 2)]
        x = sum(term.astype(F32) for term in terms).astype(BF)
    return x


def contribute_kernel(blocks, ranks_ref, acts_ref, grad_ref, a_ref, b_ref):
    for n in range(blocks):
        rows = pl.ds(n * BLOCK, BLOCK)
        a_ref[n] = (
            SCALE * jnp.dot(ranks_ref[n], acts_ref[rows, :], preferred_element_type=F32)
        ).astype(BF)
        b_ref[n] = (
            SCALE * jnp.dot(ranks_ref[blocks + n], grad_ref[rows, :], preferred_element_type=F32)
        ).astype(BF)


def contribute(ranks, acts, grad):
    blocks, rank, width = ranks.shape[0] // 2, ranks.shape[1], acts.shape[1]
    shape = jax.ShapeDtypeStruct((blocks, rank, width), BF)
    return pl.pallas_call(
        functools.partial(contribute_kernel, blocks),
        out_shape=(shape, shape),
        in_specs=[VMEM()] * 3,
        out_specs=(VMEM(),) * 2,
        compiler_params=PARAMS,
        cost_estimate=pl.CostEstimate(flops=0, bytes_accessed=8 * 2**20, transcendentals=0),
        name="factor_contributions",
    )(ranks, acts, grad)


def total_kernel(needs, *refs):
    place, used, refs = refs[0], refs[1], refs[2:]
    a_refs, b_refs = refs[:7], refs[7:14]
    mine_ref, other_ref, hold_a, hold_b, sems = refs[14:]
    copies = fetch(a_refs, hold_a, sems, 0) + fetch(b_refs, hold_b, sems, 7)
    for copy in copies:
        copy.wait()

    def one(need, hold):
        def term(source):
            at = need * 8 + source
            return hold[place[at]].astype(F32) * used[at].astype(F32)

        value = term(0)
        for source in range(1, 7):
            value += term(source)
        return value

    @pl.loop(0, needs)
    def _(need):
        mine_ref[need] = one(need, hold_a)
        mine_ref[needs + need] = one(need, hold_b)
        other_ref[need] = one(needs + need, hold_a)
        other_ref[needs + need] = one(needs + need, hold_b)


def total(place, used, parts_a, parts_b, needs):
    blocks, (rank, width) = 7 * parts_a[0].shape[0], parts_a[0].shape[1:]
    shape = jax.ShapeDtypeStruct((2 * needs, rank, width), F32)
    return pl.pallas_call(
        functools.partial(total_kernel, needs),
        out_shape=(shape, shape),
        in_specs=[SMEM()] * 2 + [ANY()] * 14,
        out_specs=(VMEM(),) * 2,
        scratch_shapes=[
            pltpu.VMEM((blocks, rank, width), BF),
            pltpu.VMEM((blocks, rank, width), BF),
            pltpu.SemaphoreType.DMA((14,)),
        ],
        compiler_params=PARAMS,
        cost_estimate=pl.CostEstimate(flops=0, bytes_accessed=16 * 2**20, transcendentals=0),
        name="gradient_totals",
    )(place, used, *parts_a, *parts_b)


def far_term(place, used, far_ref, need, first):
    at = need * 8 + 7
    return far_ref[place[at] - first].astype(F32) * used[at].astype(F32)


def share_kernel(needs, first, place, used, far_a, far_b, near_ref, out_ref):
    @pl.loop(0, needs)
    def _(need):
        for k, far in enumerate((far_a, far_b)):
            at = k * needs + need
            out_ref[at] = (
                near_ref[at] + far_term(place, used, far, needs + need, first)
            ).astype(BF)


def share(place, used, far_a, far_b, near):
    return pl.pallas_call(
        functools.partial(share_kernel, near.shape[0] // 2, 7 * far_a.shape[0]),
        out_shape=jax.ShapeDtypeStruct(near.shape, BF),
        in_specs=[SMEM()] * 2 + [VMEM()] * 3,
        out_specs=VMEM(),
        compiler_params=PARAMS,
        cost_estimate=pl.CostEstimate(flops=0, bytes_accessed=4 * 2**20, transcendentals=0),
        name="gradient_share",
    )(place, used, far_a, far_b, near)


def update_kernel(
    slots, rolls, first, place, used, own_ref, a_ref, b_ref, mine_roll, other_roll,
    far_a, far_b, mine_ref, other_ref, new_a, new_b, roll_a, roll_b,
):
    needs = slots + rolls

    def fresh(factor, at, far):
        gradient = (
            mine_ref[at]
            + far_term(place, used, far, at % needs, first)
            + other_ref[at].astype(F32)
        )
        return (factor.astype(F32) - LEARN_RATE * gradient).astype(BF)

    for n in range(slots):
        new_a[n] = fresh(a_ref[n], n, far_a)
        new_b[n] = fresh(b_ref[n], needs + n, far_b)
    for n in range(rolls):
        own = own_ref[n] == 1
        roll_a[n] = fresh(jnp.where(own, mine_roll[n], other_roll[n]), slots + n, far_a)
        roll_b[n] = fresh(
            jnp.where(own, mine_roll[rolls + n], other_roll[rolls + n]), needs + slots + n, far_b
        )


def update(place, used, own, factor_a, factor_b, mine_roll, other_roll, far_a, far_b, mine, other):
    slots, rank, width = factor_a.shape
    rolls = mine_roll.shape[0] // 2
    shape = lambda n: jax.ShapeDtypeStruct((n, rank, width), BF)
    return pl.pallas_call(
        functools.partial(update_kernel, slots, rolls, 7 * far_a.shape[0]),
        out_shape=(shape(slots), shape(slots), shape(rolls), shape(rolls)),
        in_specs=[SMEM()] * 3 + [VMEM()] * 8,
        out_specs=(VMEM(),) * 4,
        compiler_params=PARAMS,
        cost_estimate=pl.CostEstimate(flops=0, bytes_accessed=8 * 2**20, transcendentals=0),
        name="update_factors",
    )(place, used, own, factor_a, factor_b, mine_roll, other_roll, far_a, far_b, mine, other)


def frozen_kernel(grad_ref, weight_ref, out_ref):
    out_ref[...] = lax.dot_general(
        grad_ref[...], weight_ref[...], (((1,), (1,)), ((), ())), preferred_element_type=F32
    ).astype(BF)


def frozen(grad, weight):
    (rows, depth), columns = grad.shape, weight.shape[0]
    tile = 1024
    return pl.pallas_call(
        frozen_kernel,
        grid=(columns // tile,),
        out_shape=jax.ShapeDtypeStruct((rows, columns), BF),
        in_specs=[
            pl.BlockSpec((rows, depth), lambda j: (0, 0)),
            pl.BlockSpec((tile, depth), lambda j: (j, 0)),
        ],
        out_specs=pl.BlockSpec((rows, tile), lambda j: (0, j)),
        compiler_params=PARAMS,
        cost_estimate=pl.CostEstimate(
            flops=2 * rows * depth * columns, bytes_accessed=24 * 2**20, transcendentals=0
        ),
        name="frozen_partial",
    )(grad, weight)


def finish_kernel(blocks, ranks_ref, chosen_ref, base_ref, out_ref):
    for n in range(blocks):
        rows = pl.ds(n * BLOCK, BLOCK)
        term = lax.dot_general(
            ranks_ref[n], chosen_ref[n], (((0,), (0,)), ((), ())), preferred_element_type=F32
        )
        out_ref[rows, :] = (base_ref[rows, :].astype(F32) + SCALE * term).astype(BF)


def finish(ranks, chosen, base):
    blocks = chosen.shape[0]
    return pl.pallas_call(
        functools.partial(finish_kernel, blocks),
        out_shape=jax.ShapeDtypeStruct(base.shape, BF),
        in_specs=[VMEM()] * 3,
        out_specs=VMEM(),
        compiler_params=PARAMS,
        cost_estimate=pl.CostEstimate(flops=0, bytes_accessed=4 * 2**20, transcendentals=0),
        name="input_gradient",
    )(ranks, chosen, base)


def per_device(
    input_acts, out_grad, base_weight, factor_a, factor_b, block_adapter, adapter_slot, rollout_map
):
    blocks = block_adapter.shape[0]
    slots = factor_a.shape[0]
    rolls = rollout_map.size
    groups = lax.axis_size("dp")
    chips = groups // CORES
    me = lax.axis_index("dp")
    chip, core = me // CORES, me % CORES

    wanted = slot_lookup(jnp.concatenate([block_adapter, rollout_map.reshape(-1)]), adapter_slot)
    other_wanted = core_swap(wanted)
    other = me ^ 1

    def places(slot_ids):
        owner = slot_ids // slots
        here = owner % CORES == core
        distance = (owner // CORES - chip + chips) % chips
        return jnp.where(here, distance * slots + slot_ids % slots, 0), here.astype(jnp.int32)

    mine_place, mine_own = places(wanted)
    other_place, _ = places(other_wanted)

    partial_value = frozen(out_grad, base_weight)
    base = lax.psum_scatter(partial_value, "tensor", scatter_dimension=1, tiled=True)

    width = factor_a.shape[2]
    ids = jnp.pad(wanted[None].astype(BF), ((0, 15), (0, width - blocks - rolls)))
    parts_a, parts_b = ring_gather(
        factor_a.reshape(-1, width), jnp.concatenate([factor_b.reshape(-1, width), ids])
    )
    mine_sel, other_sel, mine_roll, other_roll, ring_ids = select(
        jnp.concatenate([mine_place, other_place]), parts_a, parts_b, blocks, rolls, slots
    )
    got_sel = core_swap(other_sel)
    got_roll = core_swap(other_roll)
    chosen_a, rank_parts = project(mine_own[:blocks], mine_sel, got_sel, input_acts, out_grad)
    ranks = plane_sum(rank_parts)

    order = [0, 1, 2, 3, 5, 6, 7, 4]
    ring = ring_ids[:, 0, :blocks].astype(jnp.int32)
    ring = jnp.stack([ring[k] for k in order])
    own_slots = jnp.arange(slots, dtype=jnp.int32)
    need = jnp.concatenate(
        [me * slots + own_slots, wanted[blocks:], other * slots + own_slots, other_wanted[blocks:]]
    )
    match = (need[:, None, None] == ring[None]).astype(jnp.int32)
    used = jnp.sum(match, axis=2)
    at_block = jnp.sum(match * jnp.arange(blocks, dtype=jnp.int32)[None, None], axis=2)
    source = jnp.arange(chips, dtype=jnp.int32)[None, :] * blocks + at_block
    source, used = source.reshape(-1), used.reshape(-1)

    part_a, part_b = contribute(ranks, input_acts, out_grad)
    parts_a, parts_b = ring_gather(part_a, part_b)
    near = order[:7]
    mine_total, other_total = total(
        source, used, [parts_a[k] for k in near], [parts_b[k] for k in near], slots + rolls
    )
    got_total = core_swap(share(source, used, parts_a[4], parts_b[4], other_total))
    new_a, new_b, roll_a, roll_b = update(
        source, used, mine_own[blocks:], factor_a, factor_b, mine_roll, got_roll,
        parts_a[4], parts_b[4], mine_total, got_total,
    )
    return finish(ranks, chosen_a, base), new_a, new_b, roll_a, roll_b


def solution(mesh):
    return jax.shard_map(
        per_device,
        mesh=mesh,
        in_specs=(
            P("dp", "tensor"),
            P("dp", "tensor"),
            P(None, "tensor"),
            P("dp", None, "tensor"),
            P("dp", None, "tensor"),
            P("dp"),
            P(),
            P("dp", None),
        ),
        out_specs=(
            P("dp", "tensor"),
            P("dp", None, "tensor"),
            P("dp", None, "tensor"),
            P("dp", None, "tensor"),
            P("dp", None, "tensor"),
        ),
        check_vma=False,
    )
```

```python
import functools
import math

import jax
import jax.numpy as jnp
from jax import lax
from jax.experimental import pallas as pl
from jax.experimental.pallas import tpu as pltpu
from jax.sharding import PartitionSpec as P

INPUT_FEATURES = 8192
ADAPTER_RANK = 32
BLOCK = 128
CORES = 2
SIDE = 4
LEARN_RATE = 0.25
BASE_VMEM = 58 * 2**20
SCALE = 1.0 / math.sqrt(INPUT_FEATURES * ADAPTER_RANK)

BF = jnp.bfloat16
F32 = jnp.float32
SMEM = functools.partial(pl.BlockSpec, memory_space=pltpu.SMEM)
VMEM = functools.partial(pl.BlockSpec, memory_space=pltpu.VMEM)
ANY = functools.partial(pl.BlockSpec, memory_space=pl.ANY)
PARAMS = pltpu.CompilerParams(vmem_limit_bytes=32 * 2**20)


def slot_lookup(adapter_ids, adapter_slot):
    matches = adapter_ids[:, None] == jnp.arange(adapter_slot.shape[0], dtype=jnp.int32)[None, :]
    return jnp.sum(jnp.where(matches, adapter_slot[None, :], 0), axis=1)


def z_hop(x, step):
    n = lax.axis_size("dp")
    chips = n // CORES
    perm = [(d, (d // CORES + step) % chips * CORES + d % CORES) for d in range(n)]
    return lax.ppermute(x, "dp", perm)


def core_swap(x):
    n = lax.axis_size("dp")
    return lax.ppermute(x, "dp", [(d, d ^ 1) for d in range(n)])


def plane_hop(x, step, axis):
    n = lax.axis_size("tensor")
    if axis == "y":
        perm = [(t, t // SIDE * SIDE + (t + step) % SIDE) for t in range(n)]
    else:
        perm = [(t, (t + step * SIDE) % n) for t in range(n)]
    return lax.ppermute(x, "tensor", perm)


def ring_gather(p, q):
    found = []
    last = []
    for x in (p, q):
        up = down = x
        parts = {0: x}
        for step in range(1, 4):
            up, down = z_hop(up, 1), z_hop(down, -1)
            parts[8 - step], parts[step] = up, down
        found.append(parts)
        last.append((up, down))
    found[0][4] = z_hop(last[0][0], 1)
    found[1][4] = z_hop(last[1][1], -1)
    return [[parts[place] for place in range(8)] for parts in found]


def fetch(sources, target, sems, first):
    copies, row = [], 0
    for k, ref in enumerate(sources):
        rows = ref.shape[0]
        copies.append(pltpu.make_async_copy(ref, target.at[pl.ds(row, rows)], sems.at[first + k]))
        row += rows
    for copy in copies:
        copy.start()
    return copies


def pick_kernel(rank, rows, within_mine, within_other, *refs):
    a_refs, b_refs = refs[:8], refs[8:16]
    mine_ref, other_ref, ids_ref = refs[16:]
    for k in range(8):
        for ref, within in ((mine_ref, within_mine), (other_ref, within_other)):
            at = pl.ds(pl.multiple_of(within[k] * rank, rank), rank)
            ref[k] = a_refs[k][at, :]
            ref[8 + k] = b_refs[k][at, :]
        ids_ref[k] = b_refs[k][rows:, : ids_ref.shape[2]]


def pick(within_mine, within_other, parts_a, parts_b, rank):
    rows, width = parts_a[0].shape
    tall = parts_b[0].shape[0]
    shape = jax.ShapeDtypeStruct((16, rank, width), BF)
    return pl.pallas_call(
        functools.partial(pick_kernel, rank, rows),
        out_shape=(shape, shape, jax.ShapeDtypeStruct((8, tall - rows, 128), BF)),
        in_specs=[SMEM()] * 2 + [VMEM()] * 16,
        out_specs=(VMEM(),) * 3,
        compiler_params=PARAMS,
        cost_estimate=pl.CostEstimate(flops=0, bytes_accessed=6 * 2**20, transcendentals=0),
        name="pick_factors",
    )(within_mine, within_other, *parts_a, *parts_b)


def rolls_kernel(rolls, slots, rank, *refs):
    place, _, refs = refs[0], refs[1], refs[2:]
    a_refs, b_refs = refs[:8], refs[8:16]
    mine_ref, other_ref, hold_a, hold_b, sems = refs[16:]
    copies = fetch(a_refs, hold_a, sems, 0) + fetch(b_refs, hold_b, sems, 8)
    for copy in copies:
        copy.wait()
    tail = b_refs[0].shape[0] - slots * rank
    for ref, first in ((mine_ref, 0), (other_ref, rolls)):
        for n in range(rolls):
            at = place[first + n]
            ref[n] = hold_a[pl.ds(pl.multiple_of(at * rank, rank), rank), :]
            row = at * rank + at // slots * tail
            ref[rolls + n] = hold_b[pl.ds(pl.multiple_of(row, 16), rank), :]


def pick_rolls(place, token, parts_a, parts_b, rolls, slots):
    rows, width = parts_a[0].shape
    rank = rows // slots
    tall = parts_b[0].shape[0]
    shape = jax.ShapeDtypeStruct((2 * rolls, rank, width), BF)
    return pl.pallas_call(
        functools.partial(rolls_kernel, rolls, slots, rank),
        out_shape=(shape, shape),
        in_specs=[SMEM()] + [ANY()] * 17,
        out_specs=(VMEM(),) * 2,
        scratch_shapes=[
            pltpu.VMEM((8 * rows, width), BF),
            pltpu.VMEM((8 * tall, width), BF),
            pltpu.SemaphoreType.DMA((16,)),
        ],
        compiler_params=PARAMS,
        cost_estimate=pl.CostEstimate(flops=0, bytes_accessed=8 * 2**20, transcendentals=0),
        name="pick_rollouts",
    )(place, token, *parts_a, *parts_b)


def project_kernel(
    blocks, own_ref, near_ref, mine_ref, other_ref, acts_ref, grad_ref, chosen_ref, out_ref
):
    for n in range(blocks):
        own = own_ref[n] == 1
        at = near_ref[n]
        rows = pl.ds(n * BLOCK, BLOCK)
        factor_a = jnp.where(own, mine_ref[at], other_ref[at])
        factor_b = jnp.where(own, mine_ref[8 + at], other_ref[8 + at])
        chosen_ref[n] = factor_a
        contract = (((1,), (1,)), ((), ()))
        out_ref[n] = lax.dot_general(
            factor_b, grad_ref[rows, :], contract, preferred_element_type=F32
        ).astype(BF)
        out_ref[blocks + n] = lax.dot_general(
            factor_a, acts_ref[rows, :], contract, preferred_element_type=F32
        ).astype(BF)


def project(own, near, mine, other, acts, grad):
    blocks, (rank, width) = acts.shape[0] // BLOCK, mine.shape[1:]
    return pl.pallas_call(
        functools.partial(project_kernel, blocks),
        out_shape=(
            jax.ShapeDtypeStruct((blocks, rank, width), BF),
            jax.ShapeDtypeStruct((2 * blocks, rank, BLOCK), BF),
        ),
        in_specs=[SMEM()] * 2 + [VMEM()] * 4,
        out_specs=(VMEM(),) * 2,
        compiler_params=PARAMS,
        cost_estimate=pl.CostEstimate(flops=0, bytes_accessed=8 * 2**20, transcendentals=0),
        name="project_ranks",
    )(own, near, mine, other, acts, grad)


def axis_sum(x, axis):
    terms = [x] + [plane_hop(x, step, axis) for step in (1, 3, 2)]
    return sum(term.astype(F32) for term in terms).astype(BF)


def contribute_kernel(blocks, ranks_ref, acts_ref, grad_ref, a_ref, b_ref):
    for n in range(blocks):
        rows = pl.ds(n * BLOCK, BLOCK)
        a_ref[n] = (
            SCALE * jnp.dot(ranks_ref[n], acts_ref[rows, :], preferred_element_type=F32)
        ).astype(BF)
        b_ref[n] = (
            SCALE * jnp.dot(ranks_ref[blocks + n], grad_ref[rows, :], preferred_element_type=F32)
        ).astype(BF)


def contribute(ranks, acts, grad):
    blocks, rank, width = ranks.shape[0] // 2, ranks.shape[1], acts.shape[1]
    shape = jax.ShapeDtypeStruct((blocks, rank, width), BF)
    return pl.pallas_call(
        functools.partial(contribute_kernel, blocks),
        out_shape=(shape, shape),
        in_specs=[VMEM()] * 3,
        out_specs=(VMEM(),) * 2,
        compiler_params=PARAMS,
        cost_estimate=pl.CostEstimate(flops=0, bytes_accessed=8 * 2**20, transcendentals=0),
        name="factor_contributions",
    )(ranks, acts, grad)


def total_kernel(needs, *refs):
    place, used, refs = refs[0], refs[1], refs[2:]
    a_refs, b_refs = refs[:7], refs[7:14]
    mine_ref, other_ref, hold_a, hold_b, sems = refs[14:]
    copies = fetch(a_refs, hold_a, sems, 0) + fetch(b_refs, hold_b, sems, 7)
    for copy in copies:
        copy.wait()

    def one(need, hold):
        def term(source):
            at = need * 8 + source
            return hold[place[at]].astype(F32) * used[at].astype(F32)

        value = term(0)
        for source in range(1, 7):
            value += term(source)
        return value

    @pl.loop(0, needs)
    def _(need):
        mine_ref[need] = one(need, hold_a)
        mine_ref[needs + need] = one(need, hold_b)
        other_ref[need] = one(needs + need, hold_a)
        other_ref[needs + need] = one(needs + need, hold_b)


def total(place, used, parts_a, parts_b, needs):
    blocks, (rank, width) = 7 * parts_a[0].shape[0], parts_a[0].shape[1:]
    shape = jax.ShapeDtypeStruct((2 * needs, rank, width), F32)
    return pl.pallas_call(
        functools.partial(total_kernel, needs),
        out_shape=(shape, shape),
        in_specs=[SMEM()] * 2 + [ANY()] * 14,
        out_specs=(VMEM(),) * 2,
        scratch_shapes=[
            pltpu.VMEM((blocks, rank, width), BF),
            pltpu.VMEM((blocks, rank, width), BF),
            pltpu.SemaphoreType.DMA((14,)),
        ],
        compiler_params=PARAMS,
        cost_estimate=pl.CostEstimate(flops=0, bytes_accessed=16 * 2**20, transcendentals=0),
        name="gradient_totals",
    )(place, used, *parts_a, *parts_b)


def far_term(place, used, far_ref, need, first):
    at = need * 8 + 7
    return far_ref[place[at] - first].astype(F32) * used[at].astype(F32)


def share_kernel(needs, first, place, used, far_a, far_b, near_ref, out_ref):
    @pl.loop(0, needs)
    def _(need):
        for k, far in enumerate((far_a, far_b)):
            at = k * needs + need
            out_ref[at] = (
                near_ref[at] + far_term(place, used, far, needs + need, first)
            ).astype(BF)


def share(place, used, far_a, far_b, near):
    return pl.pallas_call(
        functools.partial(share_kernel, near.shape[0] // 2, 7 * far_a.shape[0]),
        out_shape=jax.ShapeDtypeStruct(near.shape, BF),
        in_specs=[SMEM()] * 2 + [VMEM()] * 3,
        out_specs=VMEM(),
        compiler_params=PARAMS,
        cost_estimate=pl.CostEstimate(flops=0, bytes_accessed=4 * 2**20, transcendentals=0),
        name="gradient_share",
    )(place, used, far_a, far_b, near)


def update_kernel(
    slots, rolls, first, place, used, own_ref, a_ref, b_ref, mine_roll, other_roll,
    far_a, far_b, mine_ref, other_ref, new_a, new_b, roll_a, roll_b,
):
    needs = slots + rolls

    def fresh(factor, at, far):
        gradient = (
            mine_ref[at]
            + far_term(place, used, far, at % needs, first)
            + other_ref[at].astype(F32)
        )
        return (factor.astype(F32) - LEARN_RATE * gradient).astype(BF)

    for n in range(slots):
        new_a[n] = fresh(a_ref[n], n, far_a)
        new_b[n] = fresh(b_ref[n], needs + n, far_b)
    for n in range(rolls):
        own = own_ref[n] == 1
        roll_a[n] = fresh(jnp.where(own, mine_roll[n], other_roll[n]), slots + n, far_a)
        roll_b[n] = fresh(
            jnp.where(own, mine_roll[rolls + n], other_roll[rolls + n]), needs + slots + n, far_b
        )


def update(place, used, own, factor_a, factor_b, mine_roll, other_roll, far_a, far_b, mine, other):
    slots, rank, width = factor_a.shape
    rolls = mine_roll.shape[0] // 2
    shape = lambda n: jax.ShapeDtypeStruct((n, rank, width), BF)
    return pl.pallas_call(
        functools.partial(update_kernel, slots, rolls, 7 * far_a.shape[0]),
        out_shape=(shape(slots), shape(slots), shape(rolls), shape(rolls)),
        in_specs=[SMEM()] * 3 + [VMEM()] * 8,
        out_specs=(VMEM(),) * 4,
        compiler_params=PARAMS,
        cost_estimate=pl.CostEstimate(flops=0, bytes_accessed=8 * 2**20, transcendentals=0),
        name="update_factors",
    )(place, used, own, factor_a, factor_b, mine_roll, other_roll, far_a, far_b, mine, other)


def product(grad, weight):
    return lax.dot_general(grad, weight, (((1,), (1,)), ((), ())), preferred_element_type=F32)


def start_kernel(first, rows, _, grad_ref, weight_ref, out_ref):
    out_ref[0] = product(grad_ref[first : first + rows, :], weight_ref[...]).astype(BF)


def add_kernel(first, rows, _, grad_ref, weight_ref, came_ref, token_ref, out_ref):
    del token_ref
    value = product(grad_ref[first : first + rows, :], weight_ref[...])
    out_ref[0] = (value + came_ref[0].astype(F32)).astype(BF)


def base_blocks(blocks, grad, weight, first, rows, came=None, skip=0, token=None):
    count, depth = blocks.shape[0], grad.shape[1]
    width = weight.shape[0] // SIDE**2
    in_specs = [
        pl.BlockSpec(grad.shape, lambda j, at: (0, 0)),
        pl.BlockSpec((width, depth), lambda j, at: (at[j], 0)),
    ]
    arrays = [grad, weight]
    if came is not None:
        in_specs.append(pl.BlockSpec((1, rows, width), lambda j, at: (j + skip, 0, 0)))
        in_specs.append(ANY())
        arrays += [came, blocks if token is None else token]
    return pl.pallas_call(
        functools.partial(start_kernel if came is None else add_kernel, first, rows),
        out_shape=jax.ShapeDtypeStruct((count, rows, width), BF),
        grid_spec=pltpu.PrefetchScalarGridSpec(
            num_scalar_prefetch=1,
            grid=(count,),
            in_specs=in_specs,
            out_specs=pl.BlockSpec((1, rows, width), lambda j, at: (j, 0, 0)),
        ),
        compiler_params=pltpu.CompilerParams(vmem_limit_bytes=BASE_VMEM),
        cost_estimate=pl.CostEstimate(
            flops=2 * rows * depth * width * count,
            bytes_accessed=2 * width * (depth + 2 * rows) * count,
            transcendentals=0,
        ),
        name="base_blocks",
    )(blocks, *arrays)


def both_ways(x, axis):
    groups, plane = lax.axis_size("dp"), lax.axis_size("tensor")
    perm = []
    for d in range(groups):
        step = 1 if d % CORES == 0 else SIDE - 1
        for t in range(plane):
            if axis == "y":
                to = t // SIDE * SIDE + (t + step) % SIDE
            else:
                to = (t + step * SIDE) % plane
            perm.append((d * plane + t, d * plane + to))
    return lax.ppermute(x, ("dp", "tensor"), perm)


class BaseSum:
    def __init__(self, grad, weight, first, rows, axes):
        self.args = (grad, weight, first, rows)
        self.axes = axes
        here = lax.axis_index("tensor")
        way = jnp.where(lax.axis_index("dp") % CORES == 0, 1, SIDE - 1)
        x, y = here // SIDE, here % SIDE

        def block(one, two):
            up, across = (one, two) if axes[0] == "x" else (two, one)
            return (x + way * up) % SIDE * SIDE + (y + way * across) % SIDE

        hop = jnp.arange(SIDE, dtype=jnp.int32)
        self.group = [block(k, hop[::-1]) for k in range(SIDE)]

    def first_step(self):
        return both_ways(base_blocks(self.group[3], *self.args), self.axes[0])

    def next_step(self, k, came, token=None):
        return both_ways(
            base_blocks(self.group[k], *self.args, came=came, token=token), self.axes[0]
        )

    def second_axis(self, came):
        axis = self.axes[1]
        mine = self.group[0]
        head = base_blocks(mine[:1], *self.args, came=came)
        rest = base_blocks(mine[1:], *self.args, came=came, skip=1)
        moving = both_ways(head[0], axis)
        for k in range(2):
            moving = both_ways((rest[k].astype(F32) + moving.astype(F32)).astype(BF), axis)
        return [rest[2], moving]


def finish_kernel(blocks, starts, ranks_ref, chosen_ref, *refs):
    out_ref = refs[-1]
    for n in range(blocks):
        term = lax.dot_general(
            ranks_ref[n], chosen_ref[n], (((0,), (0,)), ((), ())), preferred_element_type=F32
        )
        for first, rows, refs_of in starts:
            low, high = max(first, n * BLOCK), min(first + rows, (n + 1) * BLOCK)
            if low >= high:
                continue
            base = sum(refs[k][low - first : high - first, :].astype(F32) for k in refs_of)
            part = term[low - n * BLOCK : high - n * BLOCK]
            out_ref[low:high, :] = (base + SCALE * part).astype(BF)


def finish(ranks, chosen, regions):
    blocks = chosen.shape[0]
    starts, arrays, first = [], [], 0
    for parts in regions:
        rows = parts[0].shape[0]
        starts.append((first, rows, tuple(range(len(arrays), len(arrays) + len(parts)))))
        arrays += parts
        first += rows
    return pl.pallas_call(
        functools.partial(finish_kernel, blocks, starts),
        out_shape=jax.ShapeDtypeStruct((first, chosen.shape[2]), BF),
        in_specs=[VMEM()] * (2 + len(arrays)),
        out_specs=VMEM(),
        compiler_params=PARAMS,
        cost_estimate=pl.CostEstimate(flops=0, bytes_accessed=8 * 2**20, transcendentals=0),
        name="input_gradient",
    )(ranks, chosen, *arrays)


def per_device(
    input_acts, out_grad, base_weight, factor_a, factor_b, block_adapter, adapter_slot, rollout_map
):
    blocks = block_adapter.shape[0]
    slots = factor_a.shape[0]
    rolls = rollout_map.size
    groups = lax.axis_size("dp")
    chips = groups // CORES
    me = lax.axis_index("dp")
    chip, core = me // CORES, me % CORES

    wanted = slot_lookup(jnp.concatenate([block_adapter, rollout_map.reshape(-1)]), adapter_slot)
    other_wanted = core_swap(wanted)
    other = me ^ 1

    def places(slot_ids):
        owner = slot_ids // slots
        here = owner % CORES == core
        distance = (owner // CORES - chip + chips) % chips
        return jnp.where(here, distance * slots + slot_ids % slots, 0), here.astype(jnp.int32)

    mine_place, mine_own = places(wanted)
    other_place, other_own = places(other_wanted)

    def one_each(slot_ids, here):
        distance = (slot_ids // slots // CORES - chip + chips) % chips
        hit = (distance[None] == jnp.arange(chips, dtype=jnp.int32)[:, None]) & (here[None] == 1)
        return jnp.sum(jnp.where(hit, slot_ids[None] % slots, 0), axis=1)

    mine_within = one_each(wanted[:blocks], mine_own[:blocks])
    other_within = one_each(other_wanted[:blocks], other_own[:blocks])
    mine_near = (wanted[:blocks] // slots // CORES - chip + chips) % chips

    rows = out_grad.shape[0] // 2
    by_y = BaseSum(out_grad, base_weight, 0, rows, "yx")
    by_x = BaseSum(out_grad, base_weight, rows, rows, "xy")
    sum_y, sum_x = by_y.first_step(), by_x.first_step()
    sum_y, sum_x = by_y.next_step(2, sum_y), by_x.next_step(2, sum_x)

    width = factor_a.shape[2]
    ids = jnp.pad(wanted[None].astype(BF), ((0, 15), (0, width - blocks - rolls)))
    parts_a, parts_b = ring_gather(
        factor_a.reshape(-1, width), jnp.concatenate([factor_b.reshape(-1, width), ids])
    )
    mine_sel, other_sel, ring_ids = pick(
        mine_within, other_within, parts_a, parts_b, factor_a.shape[1]
    )
    got_sel = core_swap(other_sel)
    chosen_a, rank_parts = project(
        mine_own[:blocks], mine_near, mine_sel, got_sel, input_acts, out_grad
    )
    half_ranks = axis_sum(rank_parts, "y")
    sum_y = by_y.next_step(1, sum_y, half_ranks)
    ranks = axis_sum(half_ranks, "x")
    sum_x = by_x.next_step(1, sum_x, ranks)
    regions = [by_y.second_axis(sum_y), by_x.second_axis(sum_x)]
    mine_roll, other_roll = pick_rolls(
        jnp.concatenate([mine_place[blocks:], other_place[blocks:]]),
        ranks, parts_a, parts_b, rolls, slots,
    )
    got_roll = core_swap(other_roll)

    order = [0, 1, 2, 3, 5, 6, 7, 4]
    ring = ring_ids[:, 0, :blocks].astype(jnp.int32)
    ring = jnp.stack([ring[k] for k in order])
    own_slots = jnp.arange(slots, dtype=jnp.int32)
    need = jnp.concatenate(
        [me * slots + own_slots, wanted[blocks:], other * slots + own_slots, other_wanted[blocks:]]
    )
    match = (need[:, None, None] == ring[None]).astype(jnp.int32)
    used = jnp.sum(match, axis=2)
    at_block = jnp.sum(match * jnp.arange(blocks, dtype=jnp.int32)[None, None], axis=2)
    source = jnp.arange(chips, dtype=jnp.int32)[None, :] * blocks + at_block
    source, used = source.reshape(-1), used.reshape(-1)

    part_a, part_b = contribute(ranks, input_acts, out_grad)
    parts_a, parts_b = ring_gather(part_a, part_b)
    near = order[:7]
    mine_total, other_total = total(
        source, used, [parts_a[k] for k in near], [parts_b[k] for k in near], slots + rolls
    )
    got_total = core_swap(share(source, used, parts_a[4], parts_b[4], other_total))
    new_a, new_b, roll_a, roll_b = update(
        source, used, mine_own[blocks:], factor_a, factor_b, mine_roll, got_roll,
        parts_a[4], parts_b[4], mine_total, got_total,
    )
    return finish(ranks, chosen_a, regions), new_a, new_b, roll_a, roll_b


def solution(mesh):
    return jax.shard_map(
        per_device,
        mesh=mesh,
        in_specs=(
            P("dp", "tensor"),
            P("dp", "tensor"),
            P(None, "tensor"),
            P("dp", None, "tensor"),
            P("dp", None, "tensor"),
            P("dp"),
            P(),
            P("dp", None),
        ),
        out_specs=(
            P("dp", "tensor"),
            P("dp", None, "tensor"),
            P("dp", None, "tensor"),
            P("dp", None, "tensor"),
            P("dp", None, "tensor"),
        ),
        check_vma=False,
    )
```

```python
import functools
import math

import jax
import jax.numpy as jnp
from jax import lax
from jax.experimental import pallas as pl
from jax.experimental.pallas import tpu as pltpu
from jax.sharding import PartitionSpec as P

INPUT_FEATURES = 8192
ADAPTER_RANK = 32
BLOCK = 128
CORES = 2
SIDE = 4
LEARN_RATE = 0.25
TILE = 2048
BASE_VMEM = 58 * 2**20
SCALE = 1.0 / math.sqrt(INPUT_FEATURES * ADAPTER_RANK)

BF = jnp.bfloat16
F32 = jnp.float32
SMEM = functools.partial(pl.BlockSpec, memory_space=pltpu.SMEM)
VMEM = functools.partial(pl.BlockSpec, memory_space=pltpu.VMEM)
ANY = functools.partial(pl.BlockSpec, memory_space=pl.ANY)
PARAMS = pltpu.CompilerParams(vmem_limit_bytes=32 * 2**20)


def slot_lookup(adapter_ids, adapter_slot):
    matches = adapter_ids[:, None] == jnp.arange(adapter_slot.shape[0], dtype=jnp.int32)[None, :]
    return jnp.sum(jnp.where(matches, adapter_slot[None, :], 0), axis=1)


def z_hop(x, step):
    n = lax.axis_size("dp")
    chips = n // CORES
    perm = [(d, (d // CORES + step) % chips * CORES + d % CORES) for d in range(n)]
    return lax.ppermute(x, "dp", perm)


def core_swap(x):
    n = lax.axis_size("dp")
    return lax.ppermute(x, "dp", [(d, d ^ 1) for d in range(n)])


def plane_hop(x, step, axis):
    n = lax.axis_size("tensor")
    if axis == "y":
        perm = [(t, t // SIDE * SIDE + (t + step) % SIDE) for t in range(n)]
    else:
        perm = [(t, (t + step * SIDE) % n) for t in range(n)]
    return lax.ppermute(x, "tensor", perm)


def ring_gather(p, q):
    found = []
    last = []
    for x in (p, q):
        up = down = x
        parts = {0: x}
        for step in range(1, 4):
            up, down = z_hop(up, 1), z_hop(down, -1)
            parts[8 - step], parts[step] = up, down
        found.append(parts)
        last.append((up, down))
    found[0][4] = z_hop(last[0][0], 1)
    found[1][4] = z_hop(last[1][1], -1)
    return [[parts[place] for place in range(8)] for parts in found]


def fetch(sources, target, sems, first):
    copies, row = [], 0
    for k, ref in enumerate(sources):
        rows = ref.shape[0]
        copies.append(pltpu.make_async_copy(ref, target.at[pl.ds(row, rows)], sems.at[first + k]))
        row += rows
    for copy in copies:
        copy.start()
    return copies


def pick_kernel(rank, rows, within_mine, within_other, *refs):
    a_refs, b_refs = refs[:8], refs[8:16]
    mine_ref, other_ref, ids_ref = refs[16:]
    for k in range(8):
        for ref, within in ((mine_ref, within_mine), (other_ref, within_other)):
            at = pl.ds(pl.multiple_of(within[k] * rank, rank), rank)
            ref[k] = a_refs[k][at, :]
            ref[8 + k] = b_refs[k][at, :]
        ids_ref[k] = b_refs[k][rows:, : ids_ref.shape[2]]


def pick(within_mine, within_other, parts_a, parts_b, rank):
    rows, width = parts_a[0].shape
    tall = parts_b[0].shape[0]
    shape = jax.ShapeDtypeStruct((16, rank, width), BF)
    return pl.pallas_call(
        functools.partial(pick_kernel, rank, rows),
        out_shape=(shape, shape, jax.ShapeDtypeStruct((8, tall - rows, 128), BF)),
        in_specs=[SMEM()] * 2 + [VMEM()] * 16,
        out_specs=(VMEM(),) * 3,
        compiler_params=PARAMS,
        cost_estimate=pl.CostEstimate(flops=0, bytes_accessed=6 * 2**20, transcendentals=0),
        name="pick_factors",
    )(within_mine, within_other, *parts_a, *parts_b)


def rolls_kernel(rolls, slots, rank, *refs):
    place, refs = refs[0], refs[1:]
    a_refs, b_refs = refs[:8], refs[8:16]
    mine_ref, other_ref, hold_a, hold_b, sems = refs[16:]
    copies = fetch(a_refs, hold_a, sems, 0) + fetch(b_refs, hold_b, sems, 8)
    for copy in copies:
        copy.wait()
    tail = b_refs[0].shape[0] - slots * rank
    for ref, first in ((mine_ref, 0), (other_ref, rolls)):
        for n in range(rolls):
            at = place[first + n]
            ref[n] = hold_a[pl.ds(pl.multiple_of(at * rank, rank), rank), :]
            row = at * rank + at // slots * tail
            ref[rolls + n] = hold_b[pl.ds(pl.multiple_of(row, 16), rank), :]


def pick_rolls(place, parts_a, parts_b, rolls, slots):
    rows, width = parts_a[0].shape
    rank = rows // slots
    tall = parts_b[0].shape[0]
    shape = jax.ShapeDtypeStruct((2 * rolls, rank, width), BF)
    return pl.pallas_call(
        functools.partial(rolls_kernel, rolls, slots, rank),
        out_shape=(shape, shape),
        in_specs=[SMEM()] + [ANY()] * 16,
        out_specs=(VMEM(),) * 2,
        scratch_shapes=[
            pltpu.VMEM((8 * rows, width), BF),
            pltpu.VMEM((8 * tall, width), BF),
            pltpu.SemaphoreType.DMA((16,)),
        ],
        compiler_params=PARAMS,
        cost_estimate=pl.CostEstimate(flops=0, bytes_accessed=8 * 2**20, transcendentals=0),
        name="pick_rollouts",
    )(place, *parts_a, *parts_b)


def project_kernel(
    blocks, own_ref, near_ref, here_ref, mine_ref, other_ref, acts_ref, grad_ref,
    chosen_ref, *refs,
):
    out_refs, hold = refs[:SIDE], refs[SIDE]
    for n in range(blocks):
        own = own_ref[n] == 1
        at = near_ref[n]
        rows = pl.ds(n * BLOCK, BLOCK)
        factor_a = jnp.where(own, mine_ref[at], other_ref[at])
        factor_b = jnp.where(own, mine_ref[8 + at], other_ref[8 + at])
        chosen_ref[n] = factor_a
        contract = (((1,), (1,)), ((), ()))
        hold[n] = lax.dot_general(
            factor_b, grad_ref[rows, :], contract, preferred_element_type=F32
        ).astype(BF)
        hold[blocks + n] = lax.dot_general(
            factor_a, acts_ref[rows, :], contract, preferred_element_type=F32
        ).astype(BF)
    quarter = hold.shape[0] // SIDE
    for n in range(2 * blocks, hold.shape[0]):
        hold[n] = jnp.zeros(hold.shape[1:], BF)
    for step, out_ref in enumerate(out_refs):
        first = lax.rem(here_ref[0] + step, SIDE) * quarter
        for k in range(quarter):
            out_ref[k] = hold[first + k]


def project(own, near, here, mine, other, acts, grad):
    blocks, (rank, width) = acts.shape[0] // BLOCK, mine.shape[1:]
    quarter = -(-2 * blocks // SIDE)
    return pl.pallas_call(
        functools.partial(project_kernel, blocks),
        out_shape=(jax.ShapeDtypeStruct((blocks, rank, width), BF),)
        + (jax.ShapeDtypeStruct((quarter, rank, BLOCK), BF),) * SIDE,
        in_specs=[SMEM()] * 3 + [VMEM()] * 4,
        out_specs=(VMEM(),) * (1 + SIDE),
        scratch_shapes=[pltpu.VMEM((SIDE * quarter, rank, BLOCK), BF)],
        compiler_params=PARAMS,
        cost_estimate=pl.CostEstimate(flops=0, bytes_accessed=8 * 2**20, transcendentals=0),
        name="project_ranks",
    )(own, near, here, mine, other, acts, grad)


def sum_kernel(terms, *refs):
    out_ref = refs[-1]
    out_ref[...] = sum(ref[...].astype(F32) for ref in refs[:terms]).astype(BF)


def sum_after(token, terms):
    return pl.pallas_call(
        functools.partial(sum_kernel, len(terms)),
        out_shape=jax.ShapeDtypeStruct(terms[0].shape, BF),
        in_specs=[VMEM()] * len(terms) + [ANY()],
        out_specs=VMEM(),
        compiler_params=PARAMS,
        cost_estimate=pl.CostEstimate(flops=0, bytes_accessed=2**20, transcendentals=0),
        name="rank_sum",
    )(*terms, token)


def contribute_kernel(blocks, here_ref, *refs):
    parts, (acts_ref, grad_ref, ranks_ref, a_ref, b_ref, hold) = refs[:SIDE], refs[SIDE:]
    quarter = parts[0].shape[0]
    for step, part in enumerate(parts):
        first = lax.rem(here_ref[0] + SIDE - step, SIDE) * quarter
        for k in range(quarter):
            hold[first + k] = part[k]
    for n in range(blocks):
        rows = pl.ds(n * BLOCK, BLOCK)
        ranks_ref[n] = hold[n]
        a_ref[n] = (
            SCALE * jnp.dot(hold[n], acts_ref[rows, :], preferred_element_type=F32)
        ).astype(BF)
        b_ref[n] = (
            SCALE * jnp.dot(hold[blocks + n], grad_ref[rows, :], preferred_element_type=F32)
        ).astype(BF)


def contribute(here, parts, acts, grad):
    blocks, width = acts.shape[0] // BLOCK, acts.shape[1]
    quarter, rank = parts[0].shape[:2]
    shape = jax.ShapeDtypeStruct((blocks, rank, width), BF)
    return pl.pallas_call(
        functools.partial(contribute_kernel, blocks),
        out_shape=(jax.ShapeDtypeStruct((blocks, rank, BLOCK), BF), shape, shape),
        in_specs=[SMEM()] + [VMEM()] * (2 + SIDE),
        out_specs=(VMEM(),) * 3,
        scratch_shapes=[pltpu.VMEM((SIDE * quarter, rank, BLOCK), BF)],
        compiler_params=PARAMS,
        cost_estimate=pl.CostEstimate(flops=0, bytes_accessed=8 * 2**20, transcendentals=0),
        name="factor_contributions",
    )(here, *parts, acts, grad)


def total_kernel(needs, *refs):
    place, used, refs = refs[0], refs[1], refs[2:]
    a_refs, b_refs = refs[:7], refs[7:14]
    mine_ref, other_ref, hold_a, hold_b, sems = refs[14:]
    copies = fetch(a_refs, hold_a, sems, 0) + fetch(b_refs, hold_b, sems, 7)
    for copy in copies:
        copy.wait()

    def one(need, hold):
        def term(source):
            at = need * 8 + source
            return hold[place[at]].astype(F32) * used[at].astype(F32)

        value = term(0)
        for source in range(1, 7):
            value += term(source)
        return value

    @pl.loop(0, needs)
    def _(need):
        mine_ref[need] = one(need, hold_a)
        mine_ref[needs + need] = one(need, hold_b)
        other_ref[need] = one(needs + need, hold_a)
        other_ref[needs + need] = one(needs + need, hold_b)


def total(place, used, parts_a, parts_b, needs):
    blocks, (rank, width) = 7 * parts_a[0].shape[0], parts_a[0].shape[1:]
    shape = jax.ShapeDtypeStruct((2 * needs, rank, width), F32)
    return pl.pallas_call(
        functools.partial(total_kernel, needs),
        out_shape=(shape, shape),
        in_specs=[SMEM()] * 2 + [ANY()] * 14,
        out_specs=(VMEM(),) * 2,
        scratch_shapes=[
            pltpu.VMEM((blocks, rank, width), BF),
            pltpu.VMEM((blocks, rank, width), BF),
            pltpu.SemaphoreType.DMA((14,)),
        ],
        compiler_params=PARAMS,
        cost_estimate=pl.CostEstimate(flops=0, bytes_accessed=16 * 2**20, transcendentals=0),
        name="gradient_totals",
    )(place, used, *parts_a, *parts_b)


def far_term(place, used, far_ref, need, first):
    at = need * 8 + 7
    return far_ref[place[at] - first].astype(F32) * used[at].astype(F32)


def share_kernel(needs, first, place, used, far_a, far_b, near_ref, out_ref):
    @pl.loop(0, needs)
    def _(need):
        for k, far in enumerate((far_a, far_b)):
            at = k * needs + need
            out_ref[at] = (
                near_ref[at] + far_term(place, used, far, needs + need, first)
            ).astype(BF)


def share(place, used, far_a, far_b, near):
    return pl.pallas_call(
        functools.partial(share_kernel, near.shape[0] // 2, 7 * far_a.shape[0]),
        out_shape=jax.ShapeDtypeStruct(near.shape, BF),
        in_specs=[SMEM()] * 2 + [VMEM()] * 3,
        out_specs=VMEM(),
        compiler_params=PARAMS,
        cost_estimate=pl.CostEstimate(flops=0, bytes_accessed=4 * 2**20, transcendentals=0),
        name="gradient_share",
    )(place, used, far_a, far_b, near)


def update_kernel(
    slots, rolls, first, place, used, own_ref, a_ref, b_ref, mine_roll, other_roll,
    far_a, far_b, mine_ref, other_ref, new_a, new_b, roll_a, roll_b,
):
    needs = slots + rolls

    def fresh(factor, at, far):
        gradient = (
            mine_ref[at]
            + far_term(place, used, far, at % needs, first)
            + other_ref[at].astype(F32)
        )
        return (factor.astype(F32) - LEARN_RATE * gradient).astype(BF)

    for n in range(slots):
        new_a[n] = fresh(a_ref[n], n, far_a)
        new_b[n] = fresh(b_ref[n], needs + n, far_b)
    for n in range(rolls):
        own = own_ref[n] == 1
        roll_a[n] = fresh(jnp.where(own, mine_roll[n], other_roll[n]), slots + n, far_a)
        roll_b[n] = fresh(
            jnp.where(own, mine_roll[rolls + n], other_roll[rolls + n]), needs + slots + n, far_b
        )


def update(place, used, own, factor_a, factor_b, mine_roll, other_roll, far_a, far_b, mine, other):
    slots, rank, width = factor_a.shape
    rolls = mine_roll.shape[0] // 2
    shape = lambda n: jax.ShapeDtypeStruct((n, rank, width), BF)
    return pl.pallas_call(
        functools.partial(update_kernel, slots, rolls, 7 * far_a.shape[0]),
        out_shape=(shape(slots), shape(slots), shape(rolls), shape(rolls)),
        in_specs=[SMEM()] * 3 + [VMEM()] * 8,
        out_specs=(VMEM(),) * 4,
        compiler_params=PARAMS,
        cost_estimate=pl.CostEstimate(flops=0, bytes_accessed=8 * 2**20, transcendentals=0),
        name="update_factors",
    )(place, used, own, factor_a, factor_b, mine_roll, other_roll, far_a, far_b, mine, other)


def product(grad, weight):
    return lax.dot_general(grad, weight, (((1,), (1,)), ((), ())), preferred_element_type=F32)


def products_kernel(grad_ref, weight_ref, out_ref):
    value = product(grad_ref[...], weight_ref[...]).astype(BF)
    width = out_ref.shape[2]
    for k in range(out_ref.shape[0]):
        out_ref[k] = value[:, k * width : (k + 1) * width]


def products(grad, weight, blocks):
    (rows, depth), columns = grad.shape, weight.shape[0]
    width, tile = columns // blocks, TILE
    return pl.pallas_call(
        products_kernel,
        grid=(columns // tile,),
        out_shape=jax.ShapeDtypeStruct((blocks, rows, width), BF),
        in_specs=[
            pl.BlockSpec((rows, depth), lambda j: (0, 0)),
            pl.BlockSpec((tile, depth), lambda j: (j, 0)),
        ],
        out_specs=pl.BlockSpec((tile // width, rows, width), lambda j: (j, 0, 0)),
        compiler_params=pltpu.CompilerParams(vmem_limit_bytes=BASE_VMEM),
        cost_estimate=pl.CostEstimate(
            flops=2 * rows * depth * columns, bytes_accessed=24 * 2**20, transcendentals=0
        ),
        name="base_products",
    )(grad, weight)


def finish_kernel(blocks, ranks_ref, chosen_ref, base_ref, out_ref):
    for n in range(blocks):
        rows = pl.ds(n * BLOCK, BLOCK)
        term = lax.dot_general(
            ranks_ref[n], chosen_ref[n], (((0,), (0,)), ((), ())), preferred_element_type=F32
        )
        out_ref[rows, :] = (base_ref[0, rows, :].astype(F32) + SCALE * term).astype(BF)


def finish(ranks, chosen, base):
    blocks = chosen.shape[0]
    return pl.pallas_call(
        functools.partial(finish_kernel, blocks),
        out_shape=jax.ShapeDtypeStruct(base.shape[1:], BF),
        in_specs=[VMEM()] * 3,
        out_specs=VMEM(),
        compiler_params=PARAMS,
        cost_estimate=pl.CostEstimate(flops=0, bytes_accessed=4 * 2**20, transcendentals=0),
        name="input_gradient",
    )(ranks, chosen, base)


def per_device(
    input_acts, out_grad, base_weight, factor_a, factor_b, block_adapter, adapter_slot, rollout_map
):
    blocks = block_adapter.shape[0]
    slots = factor_a.shape[0]
    rolls = rollout_map.size
    groups = lax.axis_size("dp")
    chips = groups // CORES
    me = lax.axis_index("dp")
    chip, core = me // CORES, me % CORES

    wanted = slot_lookup(jnp.concatenate([block_adapter, rollout_map.reshape(-1)]), adapter_slot)
    other_wanted = core_swap(wanted)
    other = me ^ 1

    def places(slot_ids):
        owner = slot_ids // slots
        here = owner % CORES == core
        distance = (owner // CORES - chip + chips) % chips
        return jnp.where(here, distance * slots + slot_ids % slots, 0), here.astype(jnp.int32)

    mine_place, mine_own = places(wanted)
    other_place, other_own = places(other_wanted)

    def one_each(slot_ids, here):
        distance = (slot_ids // slots // CORES - chip + chips) % chips
        hit = (distance[None] == jnp.arange(chips, dtype=jnp.int32)[:, None]) & (here[None] == 1)
        return jnp.sum(jnp.where(hit, slot_ids[None] % slots, 0), axis=1)

    mine_within = one_each(wanted[:blocks], mine_own[:blocks])
    other_within = one_each(other_wanted[:blocks], other_own[:blocks])
    mine_near = (wanted[:blocks] // slots // CORES - chip + chips) % chips

    partial_value = products(out_grad, base_weight, lax.axis_size("tensor"))
    base = lax.psum_scatter(partial_value, "tensor", scatter_dimension=0, tiled=True)

    width = factor_a.shape[2]
    ids = jnp.pad(wanted[None].astype(BF), ((0, 15), (0, width - blocks - rolls)))
    parts_a, parts_b = ring_gather(
        factor_a.reshape(-1, width), jnp.concatenate([factor_b.reshape(-1, width), ids])
    )
    mine_sel, other_sel, ring_ids = pick(
        mine_within, other_within, parts_a, parts_b, factor_a.shape[1]
    )
    got_sel = core_swap(other_sel)
    here = (lax.axis_index("tensor") % SIDE).reshape(1)
    chosen_a, *rank_parts = project(
        mine_own[:blocks], mine_near, here, mine_sel, got_sel, input_acts, out_grad
    )
    mine_roll, other_roll = pick_rolls(
        jnp.concatenate([mine_place[blocks:], other_place[blocks:]]),
        parts_a, parts_b, rolls, slots,
    )
    got_roll = core_swap(other_roll)
    quarter = sum_after(
        mine_roll,
        [rank_parts[0]] + [plane_hop(rank_parts[step], step, "y") for step in range(1, SIDE)],
    )
    quarter = sum(
        term.astype(F32)
        for term in [quarter] + [plane_hop(quarter, step, "x") for step in range(1, SIDE)]
    ).astype(BF)
    ranks, part_a, part_b = contribute(
        here,
        [quarter] + [plane_hop(quarter, step, "y") for step in range(1, SIDE)],
        input_acts, out_grad,
    )

    order = [0, 1, 2, 3, 5, 6, 7, 4]
    ring = ring_ids[:, 0, :blocks].astype(jnp.int32)
    ring = jnp.stack([ring[k] for k in order])
    own_slots = jnp.arange(slots, dtype=jnp.int32)
    need = jnp.concatenate(
        [me * slots + own_slots, wanted[blocks:], other * slots + own_slots, other_wanted[blocks:]]
    )
    match = (need[:, None, None] == ring[None]).astype(jnp.int32)
    used = jnp.sum(match, axis=2)
    at_block = jnp.sum(match * jnp.arange(blocks, dtype=jnp.int32)[None, None], axis=2)
    source = jnp.arange(chips, dtype=jnp.int32)[None, :] * blocks + at_block
    source, used = source.reshape(-1), used.reshape(-1)

    parts_a, parts_b = ring_gather(part_a, part_b)
    near = order[:7]
    mine_total, other_total = total(
        source, used, [parts_a[k] for k in near], [parts_b[k] for k in near], slots + rolls
    )
    got_total = core_swap(share(source, used, parts_a[4], parts_b[4], other_total))
    new_a, new_b, roll_a, roll_b = update(
        source, used, mine_own[blocks:], factor_a, factor_b, mine_roll, got_roll,
        parts_a[4], parts_b[4], mine_total, got_total,
    )
    return finish(ranks, chosen_a, base), new_a, new_b, roll_a, roll_b


def solution(mesh):
    return jax.shard_map(
        per_device,
        mesh=mesh,
        in_specs=(
            P("dp", "tensor"),
            P("dp", "tensor"),
            P(None, "tensor"),
            P("dp", None, "tensor"),
            P("dp", None, "tensor"),
            P("dp"),
            P(),
            P("dp", None),
        ),
        out_specs=(
            P("dp", "tensor"),
            P("dp", None, "tensor"),
            P("dp", None, "tensor"),
            P("dp", None, "tensor"),
            P("dp", None, "tensor"),
        ),
        check_vma=False,
    )
```

```python
import functools
import math

import jax
import jax.numpy as jnp
from jax import lax
from jax.experimental import pallas as pl
from jax.experimental.pallas import tpu as pltpu
from jax.sharding import PartitionSpec as P

INPUT_FEATURES = 8192
ADAPTER_RANK = 32
BLOCK = 128
CORES = 2
SIDE = 4
LEARN_RATE = 0.25
TILE = 2048
BASE_VMEM = 58 * 2**20
SCALE = 1.0 / math.sqrt(INPUT_FEATURES * ADAPTER_RANK)

BF = jnp.bfloat16
F32 = jnp.float32
SMEM = functools.partial(pl.BlockSpec, memory_space=pltpu.SMEM)
VMEM = functools.partial(pl.BlockSpec, memory_space=pltpu.VMEM)
ANY = functools.partial(pl.BlockSpec, memory_space=pl.ANY)
PARAMS = pltpu.CompilerParams(vmem_limit_bytes=32 * 2**20)


def slot_lookup(adapter_ids, adapter_slot):
    matches = adapter_ids[:, None] == jnp.arange(adapter_slot.shape[0], dtype=jnp.int32)[None, :]
    return jnp.sum(jnp.where(matches, adapter_slot[None, :], 0), axis=1)


def z_hop(x, step):
    n = lax.axis_size("dp")
    chips = n // CORES
    perm = [(d, (d // CORES + step) % chips * CORES + d % CORES) for d in range(n)]
    return lax.ppermute(x, "dp", perm)


def core_swap(x):
    n = lax.axis_size("dp")
    return lax.ppermute(x, "dp", [(d, d ^ 1) for d in range(n)])


def plane_hop(x, step, axis):
    n = lax.axis_size("tensor")
    if axis == "y":
        perm = [(t, t // SIDE * SIDE + (t + step) % SIDE) for t in range(n)]
    else:
        perm = [(t, (t + step * SIDE) % n) for t in range(n)]
    return lax.ppermute(x, "tensor", perm)


def ring_gather(p, q):
    found = []
    last = []
    for x in (p, q):
        up = down = x
        parts = {0: x}
        for step in range(1, 4):
            up, down = z_hop(up, 1), z_hop(down, -1)
            parts[8 - step], parts[step] = up, down
        found.append(parts)
        last.append((up, down))
    found[0][4] = z_hop(last[0][0], 1)
    found[1][4] = z_hop(last[1][1], -1)
    return [[parts[place] for place in range(8)] for parts in found]


def pick_kernel(rank, slots, rolls, within_mine, within_other, place, *refs):
    a_refs, b_refs = refs[:8], refs[8:16]
    mine_ref, other_ref, mine_roll, other_roll, ids_ref, hold_a, hold_b = refs[16:]
    rows = slots * rank
    for k in range(8):
        for ref, within in ((mine_ref, within_mine), (other_ref, within_other)):
            at = pl.ds(pl.multiple_of(within[k] * rank, rank), rank)
            ref[k] = a_refs[k][at, :]
            ref[8 + k] = b_refs[k][at, :]
        ids_ref[k] = b_refs[k][rows:, : ids_ref.shape[2]]
        hold_a[k * rows : (k + 1) * rows, :] = a_refs[k][...]
        hold_b[k * rows : (k + 1) * rows, :] = b_refs[k][:rows, :]
    for ref, first in ((mine_roll, 0), (other_roll, rolls)):
        for n in range(rolls):
            at = pl.ds(pl.multiple_of(place[first + n] * rank, rank), rank)
            ref[n] = hold_a[at, :]
            ref[rolls + n] = hold_b[at, :]


def pick(within_mine, within_other, place, parts_a, parts_b, rank):
    rows, width = parts_a[0].shape
    tall, rolls = parts_b[0].shape[0], place.shape[0] // 2
    shape = lambda n: jax.ShapeDtypeStruct((n, rank, width), BF)
    return pl.pallas_call(
        functools.partial(pick_kernel, rank, rows // rank, rolls),
        out_shape=(
            shape(16), shape(16), shape(2 * rolls), shape(2 * rolls),
            jax.ShapeDtypeStruct((8, tall - rows, 128), BF),
        ),
        in_specs=[SMEM()] * 3 + [VMEM()] * 16,
        out_specs=(VMEM(),) * 5,
        scratch_shapes=[pltpu.VMEM((8 * rows, width), BF)] * 2,
        compiler_params=PARAMS,
        cost_estimate=pl.CostEstimate(flops=0, bytes_accessed=6 * 2**20, transcendentals=0),
        name="pick_factors",
    )(within_mine, within_other, place, *parts_a, *parts_b)


def project_kernel(
    blocks, own_ref, near_ref, here_ref, mine_ref, other_ref, acts_ref, grad_ref,
    chosen_ref, *refs,
):
    out_refs, hold = refs[:SIDE], refs[SIDE]
    for n in range(blocks):
        own = own_ref[n] == 1
        at = near_ref[n]
        rows = pl.ds(n * BLOCK, BLOCK)
        factor_a = jnp.where(own, mine_ref[at], other_ref[at])
        factor_b = jnp.where(own, mine_ref[8 + at], other_ref[8 + at])
        chosen_ref[n] = factor_a
        contract = (((1,), (1,)), ((), ()))
        hold[n] = lax.dot_general(
            factor_b, grad_ref[rows, :], contract, preferred_element_type=F32
        ).astype(BF)
        hold[blocks + n] = lax.dot_general(
            factor_a, acts_ref[rows, :], contract, preferred_element_type=F32
        ).astype(BF)
    quarter = hold.shape[0] // SIDE
    for n in range(2 * blocks, hold.shape[0]):
        hold[n] = jnp.zeros(hold.shape[1:], BF)
    for step, out_ref in enumerate(out_refs):
        first = lax.rem(here_ref[0] + step, SIDE) * quarter
        for k in range(quarter):
            out_ref[k] = hold[first + k]


def project(own, near, here, mine, other, acts, grad):
    blocks, (rank, width) = acts.shape[0] // BLOCK, mine.shape[1:]
    quarter = -(-2 * blocks // SIDE)
    return pl.pallas_call(
        functools.partial(project_kernel, blocks),
        out_shape=(jax.ShapeDtypeStruct((blocks, rank, width), BF),)
        + (jax.ShapeDtypeStruct((quarter, rank, BLOCK), BF),) * SIDE,
        in_specs=[SMEM()] * 3 + [VMEM()] * 4,
        out_specs=(VMEM(),) * (1 + SIDE),
        scratch_shapes=[pltpu.VMEM((SIDE * quarter, rank, BLOCK), BF)],
        compiler_params=PARAMS,
        cost_estimate=pl.CostEstimate(flops=0, bytes_accessed=8 * 2**20, transcendentals=0),
        name="project_ranks",
    )(own, near, here, mine, other, acts, grad)


def contribute_kernel(blocks, here_ref, *refs):
    parts, (acts_ref, grad_ref, ranks_ref, a_ref, b_ref, hold) = refs[:SIDE], refs[SIDE:]
    quarter = parts[0].shape[0]
    for step, part in enumerate(parts):
        first = lax.rem(here_ref[0] + SIDE - step, SIDE) * quarter
        for k in range(quarter):
            hold[first + k] = part[k]
    for n in range(blocks):
        rows = pl.ds(n * BLOCK, BLOCK)
        ranks_ref[n] = hold[n]
        a_ref[n] = (
            SCALE * jnp.dot(hold[n], acts_ref[rows, :], preferred_element_type=F32)
        ).astype(BF)
        b_ref[n] = (
            SCALE * jnp.dot(hold[blocks + n], grad_ref[rows, :], preferred_element_type=F32)
        ).astype(BF)


def contribute(here, parts, acts, grad):
    blocks, width = acts.shape[0] // BLOCK, acts.shape[1]
    quarter, rank = parts[0].shape[:2]
    shape = jax.ShapeDtypeStruct((blocks, rank, width), BF)
    return pl.pallas_call(
        functools.partial(contribute_kernel, blocks),
        out_shape=(jax.ShapeDtypeStruct((blocks, rank, BLOCK), BF), shape, shape),
        in_specs=[SMEM()] + [VMEM()] * (2 + SIDE),
        out_specs=(VMEM(),) * 3,
        scratch_shapes=[pltpu.VMEM((SIDE * quarter, rank, BLOCK), BF)],
        compiler_params=PARAMS,
        cost_estimate=pl.CostEstimate(flops=0, bytes_accessed=8 * 2**20, transcendentals=0),
        name="factor_contributions",
    )(here, *parts, acts, grad)


def total_kernel(needs, place, used, *refs):
    a_refs, b_refs, (mine_ref, other_ref) = refs[:7], refs[7:14], refs[14:]

    def one(need, parts):
        value = None
        for source, part in enumerate(parts):
            at = need * 8 + source
            term = part[place[at]].astype(F32) * used[at].astype(F32)
            value = term if value is None else value + term
        return value

    @pl.loop(0, needs)
    def _(need):
        mine_ref[need] = one(need, a_refs)
        mine_ref[needs + need] = one(need, b_refs)
        other_ref[need] = one(needs + need, a_refs)
        other_ref[needs + need] = one(needs + need, b_refs)


def total(place, used, parts_a, parts_b, needs):
    shape = jax.ShapeDtypeStruct((2 * needs,) + parts_a[0].shape[1:], F32)
    return pl.pallas_call(
        functools.partial(total_kernel, needs),
        out_shape=(shape, shape),
        in_specs=[SMEM()] * 2 + [VMEM()] * 14,
        out_specs=(VMEM(),) * 2,
        compiler_params=PARAMS,
        cost_estimate=pl.CostEstimate(flops=0, bytes_accessed=16 * 2**20, transcendentals=0),
        name="gradient_totals",
    )(place, used, *parts_a, *parts_b)


def far_term(place, used, far_ref, need):
    at = need * 8 + 7
    return far_ref[place[at]].astype(F32) * used[at].astype(F32)


def share_kernel(needs, place, used, far_a, far_b, near_ref, out_ref):
    @pl.loop(0, needs)
    def _(need):
        for k, far in enumerate((far_a, far_b)):
            at = k * needs + need
            out_ref[at] = (
                near_ref[at] + far_term(place, used, far, needs + need)
            ).astype(BF)


def share(place, used, far_a, far_b, near):
    return pl.pallas_call(
        functools.partial(share_kernel, near.shape[0] // 2),
        out_shape=jax.ShapeDtypeStruct(near.shape, BF),
        in_specs=[SMEM()] * 2 + [VMEM()] * 3,
        out_specs=VMEM(),
        compiler_params=PARAMS,
        cost_estimate=pl.CostEstimate(flops=0, bytes_accessed=4 * 2**20, transcendentals=0),
        name="gradient_share",
    )(place, used, far_a, far_b, near)


def update_kernel(
    slots, rolls, place, used, own_ref, a_ref, b_ref, mine_roll, other_roll,
    far_a, far_b, mine_ref, other_ref, new_a, new_b, roll_a, roll_b,
):
    needs = slots + rolls

    def fresh(factor, at, far):
        gradient = (
            mine_ref[at]
            + far_term(place, used, far, at % needs)
            + other_ref[at].astype(F32)
        )
        return (factor.astype(F32) - LEARN_RATE * gradient).astype(BF)

    for n in range(slots):
        new_a[n] = fresh(a_ref[n], n, far_a)
        new_b[n] = fresh(b_ref[n], needs + n, far_b)
    for n in range(rolls):
        own = own_ref[n] == 1
        roll_a[n] = fresh(jnp.where(own, mine_roll[n], other_roll[n]), slots + n, far_a)
        roll_b[n] = fresh(
            jnp.where(own, mine_roll[rolls + n], other_roll[rolls + n]), needs + slots + n, far_b
        )


def update(place, used, own, factor_a, factor_b, mine_roll, other_roll, far_a, far_b, mine, other):
    slots, rank, width = factor_a.shape
    rolls = mine_roll.shape[0] // 2
    shape = lambda n: jax.ShapeDtypeStruct((n, rank, width), BF)
    return pl.pallas_call(
        functools.partial(update_kernel, slots, rolls),
        out_shape=(shape(slots), shape(slots), shape(rolls), shape(rolls)),
        in_specs=[SMEM()] * 3 + [VMEM()] * 8,
        out_specs=(VMEM(),) * 4,
        compiler_params=PARAMS,
        cost_estimate=pl.CostEstimate(flops=0, bytes_accessed=8 * 2**20, transcendentals=0),
        name="update_factors",
    )(place, used, own, factor_a, factor_b, mine_roll, other_roll, far_a, far_b, mine, other)


def product(grad, weight):
    return lax.dot_general(grad, weight, (((1,), (1,)), ((), ())), preferred_element_type=F32)


def products_kernel(grad_ref, weight_ref, out_ref):
    value = product(grad_ref[...], weight_ref[...]).astype(BF)
    width = out_ref.shape[2]
    for k in range(out_ref.shape[0]):
        out_ref[k] = value[:, k * width : (k + 1) * width]


def products(grad, weight, blocks):
    (rows, depth), columns = grad.shape, weight.shape[0]
    width, tile = columns // blocks, TILE
    return pl.pallas_call(
        products_kernel,
        grid=(columns // tile,),
        out_shape=jax.ShapeDtypeStruct((blocks, rows, width), BF),
        in_specs=[
            pl.BlockSpec((rows, depth), lambda j: (0, 0)),
            pl.BlockSpec((tile, depth), lambda j: (j, 0)),
        ],
        out_specs=pl.BlockSpec((tile // width, rows, width), lambda j: (j, 0, 0)),
        compiler_params=pltpu.CompilerParams(vmem_limit_bytes=BASE_VMEM),
        cost_estimate=pl.CostEstimate(
            flops=2 * rows * depth * columns, bytes_accessed=24 * 2**20, transcendentals=0
        ),
        name="base_products",
    )(grad, weight)


def finish_kernel(blocks, ranks_ref, chosen_ref, base_ref, out_ref):
    for n in range(blocks):
        rows = pl.ds(n * BLOCK, BLOCK)
        term = lax.dot_general(
            ranks_ref[n], chosen_ref[n], (((0,), (0,)), ((), ())), preferred_element_type=F32
        )
        out_ref[rows, :] = (base_ref[0, rows, :].astype(F32) + SCALE * term).astype(BF)


def finish(ranks, chosen, base):
    blocks = chosen.shape[0]
    return pl.pallas_call(
        functools.partial(finish_kernel, blocks),
        out_shape=jax.ShapeDtypeStruct(base.shape[1:], BF),
        in_specs=[VMEM()] * 3,
        out_specs=VMEM(),
        compiler_params=PARAMS,
        cost_estimate=pl.CostEstimate(flops=0, bytes_accessed=4 * 2**20, transcendentals=0),
        name="input_gradient",
    )(ranks, chosen, base)


def per_device(
    input_acts, out_grad, base_weight, factor_a, factor_b, block_adapter, adapter_slot, rollout_map
):
    blocks = block_adapter.shape[0]
    slots = factor_a.shape[0]
    rolls = rollout_map.size
    groups = lax.axis_size("dp")
    chips = groups // CORES
    me = lax.axis_index("dp")
    chip, core = me // CORES, me % CORES

    wanted = slot_lookup(jnp.concatenate([block_adapter, rollout_map.reshape(-1)]), adapter_slot)
    other_wanted = core_swap(wanted)
    other = me ^ 1

    def places(slot_ids):
        owner = slot_ids // slots
        here = owner % CORES == core
        distance = (owner // CORES - chip + chips) % chips
        return jnp.where(here, distance * slots + slot_ids % slots, 0), here.astype(jnp.int32)

    mine_place, mine_own = places(wanted)
    other_place, other_own = places(other_wanted)

    def one_each(slot_ids, here):
        distance = (slot_ids // slots // CORES - chip + chips) % chips
        hit = (distance[None] == jnp.arange(chips, dtype=jnp.int32)[:, None]) & (here[None] == 1)
        return jnp.sum(jnp.where(hit, slot_ids[None] % slots, 0), axis=1)

    mine_within = one_each(wanted[:blocks], mine_own[:blocks])
    other_within = one_each(other_wanted[:blocks], other_own[:blocks])
    mine_near = (wanted[:blocks] // slots // CORES - chip + chips) % chips

    partial_value = products(out_grad, base_weight, lax.axis_size("tensor"))
    base = lax.psum_scatter(partial_value, "tensor", scatter_dimension=0, tiled=True)

    width = factor_a.shape[2]
    ids = jnp.pad(wanted[None].astype(BF), ((0, 15), (0, width - blocks - rolls)))
    parts_a, parts_b = ring_gather(
        factor_a.reshape(-1, width), jnp.concatenate([factor_b.reshape(-1, width), ids])
    )
    mine_sel, other_sel, mine_roll, other_roll, ring_ids = pick(
        mine_within, other_within,
        jnp.concatenate([mine_place[blocks:], other_place[blocks:]]),
        parts_a, parts_b, factor_a.shape[1],
    )
    got_sel = core_swap(other_sel)
    here = (lax.axis_index("tensor") % SIDE).reshape(1)
    chosen_a, *rank_parts = project(
        mine_own[:blocks], mine_near, here, mine_sel, got_sel, input_acts, out_grad
    )
    got_roll = core_swap(other_roll)
    quarter = rank_parts[0]
    for axis, terms in (("y", rank_parts), ("x", None)):
        terms = terms or [quarter] * SIDE
        came = [plane_hop(terms[step], step, axis) for step in range(1, SIDE)]
        quarter = sum(term.astype(F32) for term in [quarter, *came]).astype(BF)
    ranks, part_a, part_b = contribute(
        here,
        [quarter] + [plane_hop(quarter, step, "y") for step in range(1, SIDE)],
        input_acts, out_grad,
    )

    order = [0, 1, 2, 3, 5, 6, 7, 4]
    ring = ring_ids[:, 0, :blocks].astype(jnp.int32)
    ring = jnp.stack([ring[k] for k in order])
    own_slots = jnp.arange(slots, dtype=jnp.int32)
    need = jnp.concatenate(
        [me * slots + own_slots, wanted[blocks:], other * slots + own_slots, other_wanted[blocks:]]
    )
    match = (need[:, None, None] == ring[None]).astype(jnp.int32)
    used = jnp.sum(match, axis=2)
    at_block = jnp.sum(match * jnp.arange(blocks, dtype=jnp.int32)[None, None], axis=2)
    source, used = at_block.reshape(-1), used.reshape(-1)

    parts_a, parts_b = ring_gather(part_a, part_b)
    near = order[:7]
    mine_total, other_total = total(
        source, used, [parts_a[k] for k in near], [parts_b[k] for k in near], slots + rolls
    )
    got_total = core_swap(share(source, used, parts_a[4], parts_b[4], other_total))
    new_a, new_b, roll_a, roll_b = update(
        source, used, mine_own[blocks:], factor_a, factor_b, mine_roll, got_roll,
        parts_a[4], parts_b[4], mine_total, got_total,
    )
    return finish(ranks, chosen_a, base), new_a, new_b, roll_a, roll_b


def solution(mesh):
    return jax.shard_map(
        per_device,
        mesh=mesh,
        in_specs=(
            P("dp", "tensor"),
            P("dp", "tensor"),
            P(None, "tensor"),
            P("dp", None, "tensor"),
            P("dp", None, "tensor"),
            P("dp"),
            P(),
            P("dp", None),
        ),
        out_specs=(
            P("dp", "tensor"),
            P("dp", None, "tensor"),
            P("dp", None, "tensor"),
            P("dp", None, "tensor"),
            P("dp", None, "tensor"),
        ),
        check_vma=False,
    )
```

```python
import functools
import math

import jax
import jax.numpy as jnp
from jax import lax
from jax.experimental import pallas as pl
from jax.experimental.pallas import tpu as pltpu
from jax.sharding import PartitionSpec as P

INPUT_FEATURES = 8192
ADAPTER_RANK = 32
BLOCK = 128
CORES = 2
SIDE = 4
LEARN_RATE = 0.25
TILE = 2048
BASE_VMEM = 54 * 2**20
SCALE = 1.0 / math.sqrt(INPUT_FEATURES * ADAPTER_RANK)

BF = jnp.bfloat16
F32 = jnp.float32
SMEM = functools.partial(pl.BlockSpec, memory_space=pltpu.SMEM)
VMEM = functools.partial(pl.BlockSpec, memory_space=pltpu.VMEM)
ANY = functools.partial(pl.BlockSpec, memory_space=pl.ANY)
PARAMS = pltpu.CompilerParams(vmem_limit_bytes=32 * 2**20)


def slot_lookup(adapter_ids, adapter_slot):
    matches = adapter_ids[:, None] == jnp.arange(adapter_slot.shape[0], dtype=jnp.int32)[None, :]
    return jnp.sum(jnp.where(matches, adapter_slot[None, :], 0), axis=1)


def z_hop(x, step):
    n = lax.axis_size("dp")
    chips = n // CORES
    perm = [(d, (d // CORES + step) % chips * CORES + d % CORES) for d in range(n)]
    return lax.ppermute(x, "dp", perm)


def core_swap(x):
    n = lax.axis_size("dp")
    return lax.ppermute(x, "dp", [(d, d ^ 1) for d in range(n)])


def plane_hop(x, step, axis):
    n = lax.axis_size("tensor")
    if axis == "y":
        perm = [(t, t // SIDE * SIDE + (t + step) % SIDE) for t in range(n)]
    else:
        perm = [(t, (t + step * SIDE) % n) for t in range(n)]
    return lax.ppermute(x, "tensor", perm)


def ring_gather(p, q):
    found = []
    last = []
    for x in (p, q):
        up = down = x
        parts = {0: x}
        for step in range(1, 4):
            up, down = z_hop(up, 1), z_hop(down, -1)
            parts[8 - step], parts[step] = up, down
        found.append(parts)
        last.append((up, down))
    found[0][4] = z_hop(last[0][0], 1)
    found[1][4] = z_hop(last[1][1], -1)
    return [[parts[place] for place in range(8)] for parts in found]


def pick_kernel(rank, slots, rolls, within_mine, within_other, place, *refs):
    a_refs, b_refs = refs[:8], refs[8:16]
    mine_ref, other_ref, mine_roll, other_roll, ids_ref, hold_a, hold_b = refs[16:]
    rows = slots * rank
    for k in range(8):
        for ref, within in ((mine_ref, within_mine), (other_ref, within_other)):
            at = pl.ds(pl.multiple_of(within[k] * rank, rank), rank)
            ref[k] = a_refs[k][at, :]
            ref[8 + k] = b_refs[k][at, :]
        ids_ref[k] = b_refs[k][rows:, : ids_ref.shape[2]]
        hold_a[k * rows : (k + 1) * rows, :] = a_refs[k][...]
        hold_b[k * rows : (k + 1) * rows, :] = b_refs[k][:rows, :]
    for ref, first in ((mine_roll, 0), (other_roll, rolls)):
        for n in range(rolls):
            at = pl.ds(pl.multiple_of(place[first + n] * rank, rank), rank)
            ref[n] = hold_a[at, :]
            ref[rolls + n] = hold_b[at, :]


def pick(within_mine, within_other, place, parts_a, parts_b, rank):
    rows, width = parts_a[0].shape
    tall, rolls = parts_b[0].shape[0], place.shape[0] // 2
    shape = lambda n: jax.ShapeDtypeStruct((n, rank, width), BF)
    return pl.pallas_call(
        functools.partial(pick_kernel, rank, rows // rank, rolls),
        out_shape=(
            shape(16), shape(16), shape(2 * rolls), shape(2 * rolls),
            jax.ShapeDtypeStruct((8, tall - rows, 128), BF),
        ),
        in_specs=[SMEM()] * 3 + [VMEM()] * 16,
        out_specs=(VMEM(),) * 5,
        scratch_shapes=[pltpu.VMEM((8 * rows, width), BF)] * 2,
        compiler_params=PARAMS,
        cost_estimate=pl.CostEstimate(flops=0, bytes_accessed=6 * 2**20, transcendentals=0),
        name="pick_factors",
    )(within_mine, within_other, place, *parts_a, *parts_b)


def project_kernel(
    blocks, own_ref, near_ref, here_ref, mine_ref, other_ref, acts_ref, grad_ref,
    chosen_ref, *refs,
):
    out_refs, hold = refs[:SIDE], refs[SIDE]
    for n in range(blocks):
        own = own_ref[n] == 1
        at = near_ref[n]
        rows = pl.ds(n * BLOCK, BLOCK)
        factor_a = jnp.where(own, mine_ref[at], other_ref[at])
        factor_b = jnp.where(own, mine_ref[8 + at], other_ref[8 + at])
        chosen_ref[n] = factor_a
        contract = (((1,), (1,)), ((), ()))
        hold[n] = lax.dot_general(
            factor_b, grad_ref[rows, :], contract, preferred_element_type=F32
        ).astype(BF)
        hold[blocks + n] = lax.dot_general(
            factor_a, acts_ref[rows, :], contract, preferred_element_type=F32
        ).astype(BF)
    quarter = hold.shape[0] // SIDE
    for n in range(2 * blocks, hold.shape[0]):
        hold[n] = jnp.zeros(hold.shape[1:], BF)
    for step, out_ref in enumerate(out_refs):
        first = lax.rem(here_ref[0] + step, SIDE) * quarter
        for k in range(quarter):
            out_ref[k] = hold[first + k]


def project(own, near, here, mine, other, acts, grad):
    blocks, (rank, width) = acts.shape[0] // BLOCK, mine.shape[1:]
    quarter = -(-2 * blocks // SIDE)
    return pl.pallas_call(
        functools.partial(project_kernel, blocks),
        out_shape=(jax.ShapeDtypeStruct((blocks, rank, width), BF),)
        + (jax.ShapeDtypeStruct((quarter, rank, BLOCK), BF),) * SIDE,
        in_specs=[SMEM()] * 3 + [VMEM()] * 4,
        out_specs=(VMEM(),) * (1 + SIDE),
        scratch_shapes=[pltpu.VMEM((SIDE * quarter, rank, BLOCK), BF)],
        compiler_params=PARAMS,
        cost_estimate=pl.CostEstimate(flops=0, bytes_accessed=8 * 2**20, transcendentals=0),
        name="project_ranks",
    )(own, near, here, mine, other, acts, grad)


def contribute_kernel(blocks, here_ref, *refs):
    parts, (acts_ref, grad_ref, ranks_ref, a_ref, b_ref, hold) = refs[:SIDE], refs[SIDE:]
    quarter = parts[0].shape[0]
    for step, part in enumerate(parts):
        first = lax.rem(here_ref[0] + SIDE - step, SIDE) * quarter
        for k in range(quarter):
            hold[first + k] = part[k]
    for n in range(blocks):
        rows = pl.ds(n * BLOCK, BLOCK)
        ranks_ref[n] = hold[n]
        a_ref[n] = (
            SCALE * jnp.dot(hold[n], acts_ref[rows, :], preferred_element_type=F32)
        ).astype(BF)
        b_ref[n] = (
            SCALE * jnp.dot(hold[blocks + n], grad_ref[rows, :], preferred_element_type=F32)
        ).astype(BF)


def contribute(here, parts, acts, grad):
    blocks, width = acts.shape[0] // BLOCK, acts.shape[1]
    quarter, rank = parts[0].shape[:2]
    shape = jax.ShapeDtypeStruct((blocks, rank, width), BF)
    return pl.pallas_call(
        functools.partial(contribute_kernel, blocks),
        out_shape=(jax.ShapeDtypeStruct((blocks, rank, BLOCK), BF), shape, shape),
        in_specs=[SMEM()] + [VMEM()] * (2 + SIDE),
        out_specs=(VMEM(),) * 3,
        scratch_shapes=[pltpu.VMEM((SIDE * quarter, rank, BLOCK), BF)],
        compiler_params=PARAMS,
        cost_estimate=pl.CostEstimate(flops=0, bytes_accessed=8 * 2**20, transcendentals=0),
        name="factor_contributions",
    )(here, *parts, acts, grad)


def total_kernel(needs, place, used, *refs):
    a_refs, b_refs, (_, mine_ref, other_ref) = refs[:7], refs[7:14], refs[14:]

    def one(need, parts):
        value = None
        for source, part in enumerate(parts):
            at = need * 8 + source
            term = part[place[at]].astype(F32) * used[at].astype(F32)
            value = term if value is None else value + term
        return value

    @pl.loop(0, needs)
    def _(need):
        mine_ref[need] = one(need, a_refs)
        mine_ref[needs + need] = one(need, b_refs)
        other_ref[need] = one(needs + need, a_refs)
        other_ref[needs + need] = one(needs + need, b_refs)


def total(place, used, parts_a, parts_b, token, needs):
    shape = jax.ShapeDtypeStruct((2 * needs,) + parts_a[0].shape[1:], F32)
    return pl.pallas_call(
        functools.partial(total_kernel, needs),
        out_shape=(shape, shape),
        in_specs=[SMEM()] * 2 + [VMEM()] * 15,
        out_specs=(VMEM(),) * 2,
        compiler_params=PARAMS,
        cost_estimate=pl.CostEstimate(flops=0, bytes_accessed=16 * 2**20, transcendentals=0),
        name="gradient_totals",
    )(place, used, *parts_a, *parts_b, token)


def far_term(place, used, far_ref, need):
    at = need * 8 + 7
    return far_ref[place[at]].astype(F32) * used[at].astype(F32)


def share_kernel(needs, place, used, far_a, far_b, near_ref, out_ref):
    @pl.loop(0, needs)
    def _(need):
        for k, far in enumerate((far_a, far_b)):
            at = k * needs + need
            out_ref[at] = (
                near_ref[at] + far_term(place, used, far, needs + need)
            ).astype(BF)


def share(place, used, far_a, far_b, near):
    return pl.pallas_call(
        functools.partial(share_kernel, near.shape[0] // 2),
        out_shape=jax.ShapeDtypeStruct(near.shape, BF),
        in_specs=[SMEM()] * 2 + [VMEM()] * 3,
        out_specs=VMEM(),
        compiler_params=PARAMS,
        cost_estimate=pl.CostEstimate(flops=0, bytes_accessed=4 * 2**20, transcendentals=0),
        name="gradient_share",
    )(place, used, far_a, far_b, near)


def update_kernel(
    slots, rolls, place, used, own_ref, a_ref, b_ref, mine_roll, other_roll,
    far_a, far_b, mine_ref, other_ref, new_a, new_b, roll_a, roll_b,
):
    needs = slots + rolls

    def fresh(factor, at, far):
        gradient = (
            mine_ref[at]
            + far_term(place, used, far, at % needs)
            + other_ref[at].astype(F32)
        )
        return (factor.astype(F32) - LEARN_RATE * gradient).astype(BF)

    for n in range(slots):
        new_a[n] = fresh(a_ref[n], n, far_a)
        new_b[n] = fresh(b_ref[n], needs + n, far_b)
    for n in range(rolls):
        own = own_ref[n] == 1
        roll_a[n] = fresh(jnp.where(own, mine_roll[n], other_roll[n]), slots + n, far_a)
        roll_b[n] = fresh(
            jnp.where(own, mine_roll[rolls + n], other_roll[rolls + n]), needs + slots + n, far_b
        )


def update(place, used, own, factor_a, factor_b, mine_roll, other_roll, far_a, far_b, mine, other):
    slots, rank, width = factor_a.shape
    rolls = mine_roll.shape[0] // 2
    shape = lambda n: jax.ShapeDtypeStruct((n, rank, width), BF)
    return pl.pallas_call(
        functools.partial(update_kernel, slots, rolls),
        out_shape=(shape(slots), shape(slots), shape(rolls), shape(rolls)),
        in_specs=[SMEM()] * 3 + [VMEM()] * 8,
        out_specs=(VMEM(),) * 4,
        compiler_params=PARAMS,
        cost_estimate=pl.CostEstimate(flops=0, bytes_accessed=8 * 2**20, transcendentals=0),
        name="update_factors",
    )(place, used, own, factor_a, factor_b, mine_roll, other_roll, far_a, far_b, mine, other)


def product(grad, weight):
    return lax.dot_general(grad, weight, (((1,), (1,)), ((), ())), preferred_element_type=F32)


def products_kernel(grad_ref, weight_ref, out_ref):
    value = product(grad_ref[...], weight_ref[...]).astype(BF)
    width = out_ref.shape[2]
    for k in range(out_ref.shape[0]):
        out_ref[k] = value[:, k * width : (k + 1) * width]


def products(grad, weight, blocks):
    (rows, depth), columns = grad.shape, weight.shape[0]
    width, tile = columns // blocks, TILE
    return pl.pallas_call(
        products_kernel,
        grid=(columns // tile,),
        out_shape=jax.ShapeDtypeStruct((blocks, rows, width), BF),
        in_specs=[
            pl.BlockSpec((rows, depth), lambda j: (0, 0)),
            pl.BlockSpec((tile, depth), lambda j: (j, 0)),
        ],
        out_specs=pl.BlockSpec((tile // width, rows, width), lambda j: (j, 0, 0)),
        compiler_params=pltpu.CompilerParams(vmem_limit_bytes=BASE_VMEM),
        cost_estimate=pl.CostEstimate(
            flops=2 * rows * depth * columns, bytes_accessed=24 * 2**20, transcendentals=0
        ),
        name="base_products",
    )(grad, weight)


def finish_kernel(ranks_ref, chosen_ref, base_ref, out_ref):
    for n in range(ranks_ref.shape[0]):
        rows = pl.ds(n * BLOCK, BLOCK)
        term = lax.dot_general(
            ranks_ref[n], chosen_ref[n], (((0,), (0,)), ((), ())), preferred_element_type=F32
        )
        out_ref[rows, :] = (base_ref[0, rows, :].astype(F32) + SCALE * term).astype(BF)


def finish(ranks, chosen, base):
    blocks, rank, width = chosen.shape
    return pl.pallas_call(
        finish_kernel,
        grid=(blocks,),
        out_shape=jax.ShapeDtypeStruct(base.shape[1:], BF),
        in_specs=[
            pl.BlockSpec((1, rank, BLOCK), lambda n: (n, 0, 0)),
            pl.BlockSpec((1, rank, width), lambda n: (n, 0, 0)),
            pl.BlockSpec((1, BLOCK, width), lambda n: (0, n, 0)),
        ],
        out_specs=pl.BlockSpec((BLOCK, width), lambda n: (n, 0)),
        compiler_params=pltpu.CompilerParams(vmem_limit_bytes=BASE_VMEM),
        cost_estimate=pl.CostEstimate(flops=0, bytes_accessed=4 * 2**20, transcendentals=0),
        name="input_gradient",
    )(ranks, chosen, base)


def per_device(
    input_acts, out_grad, base_weight, factor_a, factor_b, block_adapter, adapter_slot, rollout_map
):
    blocks = block_adapter.shape[0]
    slots = factor_a.shape[0]
    rolls = rollout_map.size
    groups = lax.axis_size("dp")
    chips = groups // CORES
    me = lax.axis_index("dp")
    chip, core = me // CORES, me % CORES

    wanted = slot_lookup(jnp.concatenate([block_adapter, rollout_map.reshape(-1)]), adapter_slot)
    other_wanted = core_swap(wanted)
    other = me ^ 1

    def places(slot_ids):
        owner = slot_ids // slots
        here = owner % CORES == core
        distance = (owner // CORES - chip + chips) % chips
        return jnp.where(here, distance * slots + slot_ids % slots, 0), here.astype(jnp.int32)

    mine_place, mine_own = places(wanted)
    other_place, other_own = places(other_wanted)

    def one_each(slot_ids, here):
        distance = (slot_ids // slots // CORES - chip + chips) % chips
        hit = (distance[None] == jnp.arange(chips, dtype=jnp.int32)[:, None]) & (here[None] == 1)
        return jnp.sum(jnp.where(hit, slot_ids[None] % slots, 0), axis=1)

    mine_within = one_each(wanted[:blocks], mine_own[:blocks])
    other_within = one_each(other_wanted[:blocks], other_own[:blocks])
    mine_near = (wanted[:blocks] // slots // CORES - chip + chips) % chips

    partial_value = products(out_grad, base_weight, lax.axis_size("tensor"))
    base = lax.psum_scatter(partial_value, "tensor", scatter_dimension=0, tiled=True)

    width = factor_a.shape[2]
    ids = jnp.pad(wanted[None].astype(BF), ((0, 15), (0, width - blocks - rolls)))
    parts_a, parts_b = ring_gather(
        factor_a.reshape(-1, width), jnp.concatenate([factor_b.reshape(-1, width), ids])
    )
    mine_sel, other_sel, mine_roll, other_roll, ring_ids = pick(
        mine_within, other_within,
        jnp.concatenate([mine_place[blocks:], other_place[blocks:]]),
        parts_a, parts_b, factor_a.shape[1],
    )
    got_sel = core_swap(other_sel)
    here = (lax.axis_index("tensor") % SIDE).reshape(1)
    chosen_a, *rank_parts = project(
        mine_own[:blocks], mine_near, here, mine_sel, got_sel, input_acts, out_grad
    )
    got_roll = core_swap(other_roll)
    quarter = rank_parts[0]
    for axis, terms in (("y", rank_parts), ("x", None)):
        terms = terms or [quarter] * SIDE
        came = [plane_hop(terms[step], step, axis) for step in range(1, SIDE)]
        quarter = sum(term.astype(F32) for term in [quarter, *came]).astype(BF)
    ranks, part_a, part_b = contribute(
        here,
        [quarter] + [plane_hop(quarter, step, "y") for step in range(1, SIDE)],
        input_acts, out_grad,
    )

    order = [0, 1, 2, 3, 5, 6, 7, 4]
    ring = ring_ids[:, 0, :blocks].astype(jnp.int32)
    ring = jnp.stack([ring[k] for k in order])
    own_slots = jnp.arange(slots, dtype=jnp.int32)
    need = jnp.concatenate(
        [me * slots + own_slots, wanted[blocks:], other * slots + own_slots, other_wanted[blocks:]]
    )
    match = (need[:, None, None] == ring[None]).astype(jnp.int32)
    used = jnp.sum(match, axis=2)
    at_block = jnp.sum(match * jnp.arange(blocks, dtype=jnp.int32)[None, None], axis=2)
    source, used = at_block.reshape(-1), used.reshape(-1)

    parts_a, parts_b = ring_gather(part_a, part_b)
    near = order[:7]
    mine_total, other_total = total(
        source, used, [parts_a[k] for k in near], [parts_b[k] for k in near], got_roll, slots + rolls
    )
    got_total = core_swap(share(source, used, parts_a[4], parts_b[4], other_total))
    new_a, new_b, roll_a, roll_b = update(
        source, used, mine_own[blocks:], factor_a, factor_b, mine_roll, got_roll,
        parts_a[4], parts_b[4], mine_total, got_total,
    )
    return finish(ranks, chosen_a, base), new_a, new_b, roll_a, roll_b


def solution(mesh):
    return jax.shard_map(
        per_device,
        mesh=mesh,
        in_specs=(
            P("dp", "tensor"),
            P("dp", "tensor"),
            P(None, "tensor"),
            P("dp", None, "tensor"),
            P("dp", None, "tensor"),
            P("dp"),
            P(),
            P("dp", None),
        ),
        out_specs=(
            P("dp", "tensor"),
            P("dp", None, "tensor"),
            P("dp", None, "tensor"),
            P("dp", None, "tensor"),
            P("dp", None, "tensor"),
        ),
        check_vma=False,
    )
```

```python
import functools
import math

import jax
import jax.numpy as jnp
from jax import lax
from jax.experimental import pallas as pl
from jax.experimental.pallas import tpu as pltpu
from jax.sharding import PartitionSpec as P

INPUT_FEATURES = 8192
ADAPTER_RANK = 32
BLOCK = 128
CORES = 2
SIDE = 4
LEARN_RATE = 0.25
TILE = 2048
BASE_VMEM = 58 * 2**20
SCALE = 1.0 / math.sqrt(INPUT_FEATURES * ADAPTER_RANK)

BF = jnp.bfloat16
F32 = jnp.float32
SMEM = functools.partial(pl.BlockSpec, memory_space=pltpu.SMEM)
VMEM = functools.partial(pl.BlockSpec, memory_space=pltpu.VMEM)
ANY = functools.partial(pl.BlockSpec, memory_space=pl.ANY)
PARAMS = pltpu.CompilerParams(vmem_limit_bytes=32 * 2**20)


def slot_lookup(adapter_ids, adapter_slot):
    matches = adapter_ids[:, None] == jnp.arange(adapter_slot.shape[0], dtype=jnp.int32)[None, :]
    return jnp.sum(jnp.where(matches, adapter_slot[None, :], 0), axis=1)


def z_hop(x, step):
    n = lax.axis_size("dp")
    chips = n // CORES
    perm = [(d, (d // CORES + step) % chips * CORES + d % CORES) for d in range(n)]
    return lax.ppermute(x, "dp", perm)


def core_swap(x):
    n = lax.axis_size("dp")
    return lax.ppermute(x, "dp", [(d, d ^ 1) for d in range(n)])


def plane_hop(x, step, axis):
    n = lax.axis_size("tensor")
    if axis == "y":
        perm = [(t, t // SIDE * SIDE + (t + step) % SIDE) for t in range(n)]
    else:
        perm = [(t, (t + step * SIDE) % n) for t in range(n)]
    return lax.ppermute(x, "tensor", perm)


def ring_gather(p, q):
    found = []
    last = []
    for x in (p, q):
        up = down = x
        parts = {0: x}
        for step in range(1, 4):
            up, down = z_hop(up, 1), z_hop(down, -1)
            parts[8 - step], parts[step] = up, down
        found.append(parts)
        last.append((up, down))
    found[0][4] = z_hop(last[0][0], 1)
    found[1][4] = z_hop(last[1][1], -1)
    return [[parts[place] for place in range(8)] for parts in found]


def pick_kernel(rank, slots, rolls, within_mine, within_other, place, *refs):
    a_refs, b_refs = refs[:8], refs[8:16]
    mine_ref, other_ref, mine_roll, other_roll, ids_ref, hold_a, hold_b = refs[16:]
    rows = slots * rank
    for k in range(8):
        for ref, within in ((mine_ref, within_mine), (other_ref, within_other)):
            at = pl.ds(pl.multiple_of(within[k] * rank, rank), rank)
            ref[k] = a_refs[k][at, :]
            ref[8 + k] = b_refs[k][at, :]
        ids_ref[k] = b_refs[k][rows:, : ids_ref.shape[2]]
        hold_a[k * rows : (k + 1) * rows, :] = a_refs[k][...]
        hold_b[k * rows : (k + 1) * rows, :] = b_refs[k][:rows, :]
    for ref, first in ((mine_roll, 0), (other_roll, rolls)):
        for n in range(rolls):
            at = pl.ds(pl.multiple_of(place[first + n] * rank, rank), rank)
            ref[n] = hold_a[at, :]
            ref[rolls + n] = hold_b[at, :]


def pick(within_mine, within_other, place, parts_a, parts_b, rank):
    rows, width = parts_a[0].shape
    tall, rolls = parts_b[0].shape[0], place.shape[0] // 2
    shape = lambda n: jax.ShapeDtypeStruct((n, rank, width), BF)
    return pl.pallas_call(
        functools.partial(pick_kernel, rank, rows // rank, rolls),
        out_shape=(
            shape(16), shape(16), shape(2 * rolls), shape(2 * rolls),
            jax.ShapeDtypeStruct((8, tall - rows, 128), BF),
        ),
        in_specs=[SMEM()] * 3 + [VMEM()] * 16,
        out_specs=(VMEM(),) * 5,
        scratch_shapes=[pltpu.VMEM((8 * rows, width), BF)] * 2,
        compiler_params=PARAMS,
        cost_estimate=pl.CostEstimate(flops=0, bytes_accessed=6 * 2**20, transcendentals=0),
        name="pick_factors",
    )(within_mine, within_other, place, *parts_a, *parts_b)


def project_kernel(
    blocks, own_ref, near_ref, here_ref, mine_ref, other_ref, acts_ref, grad_ref,
    chosen_ref, *refs,
):
    out_refs, hold = refs[:SIDE], refs[SIDE]
    for n in range(blocks):
        own = own_ref[n] == 1
        at = near_ref[n]
        rows = pl.ds(n * BLOCK, BLOCK)
        factor_a = jnp.where(own, mine_ref[at], other_ref[at])
        factor_b = jnp.where(own, mine_ref[8 + at], other_ref[8 + at])
        chosen_ref[n] = factor_a
        contract = (((1,), (1,)), ((), ()))
        hold[n] = lax.dot_general(
            factor_b, grad_ref[rows, :], contract, preferred_element_type=F32
        ).astype(BF)
        hold[blocks + n] = lax.dot_general(
            factor_a, acts_ref[rows, :], contract, preferred_element_type=F32
        ).astype(BF)
    quarter = hold.shape[0] // SIDE
    for n in range(2 * blocks, hold.shape[0]):
        hold[n] = jnp.zeros(hold.shape[1:], BF)
    for step, out_ref in enumerate(out_refs):
        first = lax.rem(here_ref[0] + step, SIDE) * quarter
        for k in range(quarter):
            out_ref[k] = hold[first + k]


def project(own, near, here, mine, other, acts, grad):
    blocks, (rank, width) = acts.shape[0] // BLOCK, mine.shape[1:]
    quarter = -(-2 * blocks // SIDE)
    return pl.pallas_call(
        functools.partial(project_kernel, blocks),
        out_shape=(jax.ShapeDtypeStruct((blocks, rank, width), BF),)
        + (jax.ShapeDtypeStruct((quarter, rank, BLOCK), BF),) * SIDE,
        in_specs=[SMEM()] * 3 + [VMEM()] * 4,
        out_specs=(VMEM(),) * (1 + SIDE),
        scratch_shapes=[pltpu.VMEM((SIDE * quarter, rank, BLOCK), BF)],
        compiler_params=PARAMS,
        cost_estimate=pl.CostEstimate(flops=0, bytes_accessed=8 * 2**20, transcendentals=0),
        name="project_ranks",
    )(own, near, here, mine, other, acts, grad)


def contribute_kernel(blocks, here_ref, *refs):
    parts, (acts_ref, grad_ref, ranks_ref, a_ref, b_ref, hold) = refs[:SIDE], refs[SIDE:]
    quarter = parts[0].shape[0]
    for step, part in enumerate(parts):
        first = lax.rem(here_ref[0] + SIDE - step, SIDE) * quarter
        for k in range(quarter):
            hold[first + k] = part[k]
    for n in range(blocks):
        rows = pl.ds(n * BLOCK, BLOCK)
        ranks_ref[n] = hold[n]
        a_ref[n] = (
            SCALE * jnp.dot(hold[n], acts_ref[rows, :], preferred_element_type=F32)
        ).astype(BF)
        b_ref[n] = (
            SCALE * jnp.dot(hold[blocks + n], grad_ref[rows, :], preferred_element_type=F32)
        ).astype(BF)


def contribute(here, parts, acts, grad):
    blocks, width = acts.shape[0] // BLOCK, acts.shape[1]
    quarter, rank = parts[0].shape[:2]
    shape = jax.ShapeDtypeStruct((blocks, rank, width), BF)
    return pl.pallas_call(
        functools.partial(contribute_kernel, blocks),
        out_shape=(jax.ShapeDtypeStruct((blocks, rank, BLOCK), BF), shape, shape),
        in_specs=[SMEM()] + [VMEM()] * (2 + SIDE),
        out_specs=(VMEM(),) * 3,
        scratch_shapes=[pltpu.VMEM((SIDE * quarter, rank, BLOCK), BF)],
        compiler_params=PARAMS,
        cost_estimate=pl.CostEstimate(flops=0, bytes_accessed=8 * 2**20, transcendentals=0),
        name="factor_contributions",
    )(here, *parts, acts, grad)


def total_kernel(needs, place, used, *refs):
    a_refs, b_refs, (mine_ref, other_ref) = refs[:7], refs[7:14], refs[14:]

    def one(need, parts):
        value = None
        for source, part in enumerate(parts):
            at = need * 8 + source
            term = part[place[at]].astype(F32) * used[at].astype(F32)
            value = term if value is None else value + term
        return value

    @pl.loop(0, needs)
    def _(need):
        mine_ref[need] = one(need, a_refs)
        mine_ref[needs + need] = one(need, b_refs)
        other_ref[need] = one(needs + need, a_refs)
        other_ref[needs + need] = one(needs + need, b_refs)


def total(place, used, parts_a, parts_b, needs):
    shape = jax.ShapeDtypeStruct((2 * needs,) + parts_a[0].shape[1:], F32)
    return pl.pallas_call(
        functools.partial(total_kernel, needs),
        out_shape=(shape, shape),
        in_specs=[SMEM()] * 2 + [VMEM()] * 14,
        out_specs=(VMEM(),) * 2,
        compiler_params=PARAMS,
        cost_estimate=pl.CostEstimate(flops=0, bytes_accessed=16 * 2**20, transcendentals=0),
        name="gradient_totals",
    )(place, used, *parts_a, *parts_b)


def far_term(place, used, far_ref, need):
    at = need * 8 + 7
    return far_ref[place[at]].astype(F32) * used[at].astype(F32)


def share_kernel(needs, place, used, far_a, far_b, near_ref, _, out_ref):
    @pl.loop(0, needs)
    def _(need):
        for k, far in enumerate((far_a, far_b)):
            at = k * needs + need
            out_ref[at] = (
                near_ref[at] + far_term(place, used, far, needs + need)
            ).astype(BF)


def share(place, used, far_a, far_b, near, token):
    return pl.pallas_call(
        functools.partial(share_kernel, near.shape[0] // 2),
        out_shape=jax.ShapeDtypeStruct(near.shape, BF),
        in_specs=[SMEM()] * 2 + [VMEM()] * 4,
        out_specs=VMEM(),
        compiler_params=PARAMS,
        cost_estimate=pl.CostEstimate(flops=0, bytes_accessed=4 * 2**20, transcendentals=0),
        name="gradient_share",
    )(place, used, far_a, far_b, near, token)


def update_kernel(
    slots, rolls, place, used, own_ref, a_ref, b_ref, mine_roll, other_roll,
    far_a, far_b, mine_ref, other_ref, new_a, new_b, roll_a, roll_b,
):
    needs = slots + rolls

    def fresh(factor, at, far):
        gradient = (
            mine_ref[at]
            + far_term(place, used, far, at % needs)
            + other_ref[at].astype(F32)
        )
        return (factor.astype(F32) - LEARN_RATE * gradient).astype(BF)

    for n in range(slots):
        new_a[n] = fresh(a_ref[n], n, far_a)
        new_b[n] = fresh(b_ref[n], needs + n, far_b)
    for n in range(rolls):
        own = own_ref[n] == 1
        roll_a[n] = fresh(jnp.where(own, mine_roll[n], other_roll[n]), slots + n, far_a)
        roll_b[n] = fresh(
            jnp.where(own, mine_roll[rolls + n], other_roll[rolls + n]), needs + slots + n, far_b
        )


def update(place, used, own, factor_a, factor_b, mine_roll, other_roll, far_a, far_b, mine, other):
    slots, rank, width = factor_a.shape
    rolls = mine_roll.shape[0] // 2
    shape = lambda n: jax.ShapeDtypeStruct((n, rank, width), BF)
    return pl.pallas_call(
        functools.partial(update_kernel, slots, rolls),
        out_shape=(shape(slots), shape(slots), shape(rolls), shape(rolls)),
        in_specs=[SMEM()] * 3 + [VMEM()] * 8,
        out_specs=(VMEM(),) * 4,
        compiler_params=PARAMS,
        cost_estimate=pl.CostEstimate(flops=0, bytes_accessed=8 * 2**20, transcendentals=0),
        name="update_factors",
    )(place, used, own, factor_a, factor_b, mine_roll, other_roll, far_a, far_b, mine, other)


def product(grad, weight):
    return lax.dot_general(grad, weight, (((1,), (1,)), ((), ())), preferred_element_type=F32)


def products_kernel(grad_ref, weight_ref, out_ref):
    value = product(grad_ref[...], weight_ref[...]).astype(BF)
    width = out_ref.shape[2]
    for k in range(out_ref.shape[0]):
        out_ref[k] = value[:, k * width : (k + 1) * width]


def products(grad, weight, blocks):
    (rows, depth), columns = grad.shape, weight.shape[0]
    width, tile = columns // blocks, TILE
    return pl.pallas_call(
        products_kernel,
        grid=(columns // tile,),
        out_shape=jax.ShapeDtypeStruct((blocks, rows, width), BF),
        in_specs=[
            pl.BlockSpec((rows, depth), lambda j: (0, 0)),
            pl.BlockSpec((tile, depth), lambda j: (j, 0)),
        ],
        out_specs=pl.BlockSpec((tile // width, rows, width), lambda j: (j, 0, 0)),
        compiler_params=pltpu.CompilerParams(vmem_limit_bytes=BASE_VMEM),
        cost_estimate=pl.CostEstimate(
            flops=2 * rows * depth * columns, bytes_accessed=24 * 2**20, transcendentals=0
        ),
        name="base_products",
    )(grad, weight)


def finish_kernel(blocks, ranks_ref, chosen_ref, base_ref, out_ref, hold, done, came, left):
    arriving, leaving = [], []
    for n in range(blocks):
        rows = pl.ds(n * BLOCK, BLOCK)
        arriving.append(pltpu.make_async_copy(base_ref.at[rows], hold.at[rows], came.at[n]))
        leaving.append(pltpu.make_async_copy(done.at[rows], out_ref.at[rows], left.at[n]))
        arriving[n].start()
    for n in range(blocks):
        rows = pl.ds(n * BLOCK, BLOCK)
        term = lax.dot_general(
            ranks_ref[n], chosen_ref[n], (((0,), (0,)), ((), ())), preferred_element_type=F32
        )
        arriving[n].wait()
        done[rows, :] = (hold[rows, :].astype(F32) + SCALE * term).astype(BF)
        leaving[n].start()
    for n in range(blocks):
        leaving[n].wait()


def finish(ranks, chosen, base):
    blocks = chosen.shape[0]
    return pl.pallas_call(
        functools.partial(finish_kernel, blocks),
        out_shape=jax.ShapeDtypeStruct(base.shape, BF),
        in_specs=[VMEM()] * 2 + [ANY()],
        out_specs=ANY(),
        scratch_shapes=[pltpu.VMEM(base.shape, BF)] * 2
        + [pltpu.SemaphoreType.DMA((blocks,))] * 2,
        input_output_aliases={2: 0},
        compiler_params=PARAMS,
        cost_estimate=pl.CostEstimate(flops=0, bytes_accessed=4 * 2**20, transcendentals=0),
        name="input_gradient",
    )(ranks, chosen, base)


def per_device(
    input_acts, out_grad, base_weight, factor_a, factor_b, block_adapter, adapter_slot, rollout_map
):
    blocks = block_adapter.shape[0]
    slots = factor_a.shape[0]
    rolls = rollout_map.size
    groups = lax.axis_size("dp")
    chips = groups // CORES
    me = lax.axis_index("dp")
    chip, core = me // CORES, me % CORES

    wanted = slot_lookup(jnp.concatenate([block_adapter, rollout_map.reshape(-1)]), adapter_slot)
    other_wanted = core_swap(wanted)
    other = me ^ 1

    def places(slot_ids):
        owner = slot_ids // slots
        here = owner % CORES == core
        distance = (owner // CORES - chip + chips) % chips
        return jnp.where(here, distance * slots + slot_ids % slots, 0), here.astype(jnp.int32)

    mine_place, mine_own = places(wanted)
    other_place, other_own = places(other_wanted)

    def one_each(slot_ids, here):
        distance = (slot_ids // slots // CORES - chip + chips) % chips
        hit = (distance[None] == jnp.arange(chips, dtype=jnp.int32)[:, None]) & (here[None] == 1)
        return jnp.sum(jnp.where(hit, slot_ids[None] % slots, 0), axis=1)

    mine_within = one_each(wanted[:blocks], mine_own[:blocks])
    other_within = one_each(other_wanted[:blocks], other_own[:blocks])
    mine_near = (wanted[:blocks] // slots // CORES - chip + chips) % chips

    partial_value = products(out_grad, base_weight, lax.axis_size("tensor"))
    base = lax.psum_scatter(partial_value, "tensor", scatter_dimension=0, tiled=True)

    width = factor_a.shape[2]
    ids = jnp.pad(wanted[None].astype(BF), ((0, 15), (0, width - blocks - rolls)))
    parts_a, parts_b = ring_gather(
        factor_a.reshape(-1, width), jnp.concatenate([factor_b.reshape(-1, width), ids])
    )
    mine_sel, other_sel, mine_roll, other_roll, ring_ids = pick(
        mine_within, other_within,
        jnp.concatenate([mine_place[blocks:], other_place[blocks:]]),
        parts_a, parts_b, factor_a.shape[1],
    )
    got_sel = core_swap(other_sel)
    here = (lax.axis_index("tensor") % SIDE).reshape(1)
    chosen_a, *rank_parts = project(
        mine_own[:blocks], mine_near, here, mine_sel, got_sel, input_acts, out_grad
    )
    got_roll = core_swap(other_roll)
    quarter = rank_parts[0]
    for axis, terms in (("y", rank_parts), ("x", None)):
        terms = terms or [quarter] * SIDE
        came = [plane_hop(terms[step], step, axis) for step in range(1, SIDE)]
        quarter = sum(term.astype(F32) for term in [quarter, *came]).astype(BF)
    ranks, part_a, part_b = contribute(
        here,
        [quarter] + [plane_hop(quarter, step, "y") for step in range(1, SIDE)],
        input_acts, out_grad,
    )

    order = [0, 1, 2, 3, 5, 6, 7, 4]
    ring = ring_ids[:, 0, :blocks].astype(jnp.int32)
    ring = jnp.stack([ring[k] for k in order])
    own_slots = jnp.arange(slots, dtype=jnp.int32)
    need = jnp.concatenate(
        [me * slots + own_slots, wanted[blocks:], other * slots + own_slots, other_wanted[blocks:]]
    )
    match = (need[:, None, None] == ring[None]).astype(jnp.int32)
    used = jnp.sum(match, axis=2)
    at_block = jnp.sum(match * jnp.arange(blocks, dtype=jnp.int32)[None, None], axis=2)
    source, used = at_block.reshape(-1), used.reshape(-1)

    parts_a, parts_b = ring_gather(part_a, part_b)
    near = order[:7]
    mine_total, other_total = total(
        source, used, [parts_a[k] for k in near], [parts_b[k] for k in near], slots + rolls
    )
    got_total = core_swap(share(source, used, parts_a[4], parts_b[4], other_total, got_roll))
    new_a, new_b, roll_a, roll_b = update(
        source, used, mine_own[blocks:], factor_a, factor_b, mine_roll, got_roll,
        parts_a[4], parts_b[4], mine_total, got_total,
    )
    return finish(ranks, chosen_a, base[0]), new_a, new_b, roll_a, roll_b


def solution(mesh):
    return jax.shard_map(
        per_device,
        mesh=mesh,
        in_specs=(
            P("dp", "tensor"),
            P("dp", "tensor"),
            P(None, "tensor"),
            P("dp", None, "tensor"),
            P("dp", None, "tensor"),
            P("dp"),
            P(),
            P("dp", None),
        ),
        out_specs=(
            P("dp", "tensor"),
            P("dp", None, "tensor"),
            P("dp", None, "tensor"),
            P("dp", None, "tensor"),
            P("dp", None, "tensor"),
        ),
        check_vma=False,
    )
```

```python
import functools
import math

import jax
import jax.numpy as jnp
from jax import lax
from jax.experimental import pallas as pl
from jax.experimental.pallas import tpu as pltpu
from jax.sharding import PartitionSpec as P

INPUT_FEATURES = 8192
ADAPTER_RANK = 32
BLOCK = 128
CORES = 2
SIDE = 4
LEARN_RATE = 0.25
TILE = 2048
BASE_VMEM = 58 * 2**20
SCALE = 1.0 / math.sqrt(INPUT_FEATURES * ADAPTER_RANK)

BF = jnp.bfloat16
F32 = jnp.float32
SMEM = functools.partial(pl.BlockSpec, memory_space=pltpu.SMEM)
VMEM = functools.partial(pl.BlockSpec, memory_space=pltpu.VMEM)
ANY = functools.partial(pl.BlockSpec, memory_space=pl.ANY)
PARAMS = pltpu.CompilerParams(vmem_limit_bytes=32 * 2**20)


def slot_lookup(adapter_ids, adapter_slot):
    matches = adapter_ids[:, None] == jnp.arange(adapter_slot.shape[0], dtype=jnp.int32)[None, :]
    return jnp.sum(jnp.where(matches, adapter_slot[None, :], 0), axis=1)


def z_hop(x, step):
    n = lax.axis_size("dp")
    chips = n // CORES
    perm = [(d, (d // CORES + step) % chips * CORES + d % CORES) for d in range(n)]
    return lax.ppermute(x, "dp", perm)


def core_swap(x):
    n = lax.axis_size("dp")
    return lax.ppermute(x, "dp", [(d, d ^ 1) for d in range(n)])


def plane_hop(x, step, axis):
    n = lax.axis_size("tensor")
    if axis == "y":
        perm = [(t, t // SIDE * SIDE + (t + step) % SIDE) for t in range(n)]
    else:
        perm = [(t, (t + step * SIDE) % n) for t in range(n)]
    return lax.ppermute(x, "tensor", perm)


def ring_gather(p, q):
    found = []
    last = []
    for x in (p, q):
        up = down = x
        parts = {0: x}
        for step in range(1, 4):
            up, down = z_hop(up, 1), z_hop(down, -1)
            parts[8 - step], parts[step] = up, down
        found.append(parts)
        last.append((up, down))
    found[0][4] = z_hop(last[0][0], 1)
    found[1][4] = z_hop(last[1][1], -1)
    return [[parts[place] for place in range(8)] for parts in found]


def pick_kernel(rank, slots, rolls, within_mine, within_other, place, *refs):
    a_refs, b_refs = refs[:8], refs[8:16]
    mine_ref, other_ref, mine_roll, other_roll, ids_ref, hold_a, hold_b = refs[16:]
    rows = slots * rank
    for k in range(8):
        for ref, within in ((mine_ref, within_mine), (other_ref, within_other)):
            at = pl.ds(pl.multiple_of(within[k] * rank, rank), rank)
            ref[k] = a_refs[k][at, :]
            ref[8 + k] = b_refs[k][at, :]
        ids_ref[k] = b_refs[k][rows:, : ids_ref.shape[2]]
        hold_a[k * rows : (k + 1) * rows, :] = a_refs[k][...]
        hold_b[k * rows : (k + 1) * rows, :] = b_refs[k][:rows, :]
    for ref, first in ((mine_roll, 0), (other_roll, rolls)):
        for n in range(rolls):
            at = pl.ds(pl.multiple_of(place[first + n] * rank, rank), rank)
            ref[n] = hold_a[at, :]
            ref[rolls + n] = hold_b[at, :]


def pick(within_mine, within_other, place, parts_a, parts_b, rank):
    rows, width = parts_a[0].shape
    tall, rolls = parts_b[0].shape[0], place.shape[0] // 2
    shape = lambda n: jax.ShapeDtypeStruct((n, rank, width), BF)
    return pl.pallas_call(
        functools.partial(pick_kernel, rank, rows // rank, rolls),
        out_shape=(
            shape(16), shape(16), shape(2 * rolls), shape(2 * rolls),
            jax.ShapeDtypeStruct((8, tall - rows, 128), BF),
        ),
        in_specs=[SMEM()] * 3 + [VMEM()] * 16,
        out_specs=(VMEM(),) * 5,
        scratch_shapes=[pltpu.VMEM((8 * rows, width), BF)] * 2,
        compiler_params=PARAMS,
        cost_estimate=pl.CostEstimate(flops=0, bytes_accessed=6 * 2**20, transcendentals=0),
        name="pick_factors",
    )(within_mine, within_other, place, *parts_a, *parts_b)


def project_kernel(
    blocks, own_ref, near_ref, here_ref, mine_ref, other_ref, acts_ref, grad_ref,
    chosen_ref, *refs,
):
    out_refs, hold = refs[:SIDE], refs[SIDE]
    for n in range(blocks):
        own = own_ref[n] == 1
        at = near_ref[n]
        rows = pl.ds(n * BLOCK, BLOCK)
        factor_a = jnp.where(own, mine_ref[at], other_ref[at])
        factor_b = jnp.where(own, mine_ref[8 + at], other_ref[8 + at])
        chosen_ref[n] = factor_a
        contract = (((1,), (1,)), ((), ()))
        hold[n] = lax.dot_general(
            factor_b, grad_ref[rows, :], contract, preferred_element_type=F32
        ).astype(BF)
        hold[blocks + n] = lax.dot_general(
            factor_a, acts_ref[rows, :], contract, preferred_element_type=F32
        ).astype(BF)
    quarter = hold.shape[0] // SIDE
    for n in range(2 * blocks, hold.shape[0]):
        hold[n] = jnp.zeros(hold.shape[1:], BF)
    for step, out_ref in enumerate(out_refs):
        first = lax.rem(here_ref[0] + step, SIDE) * quarter
        for k in range(quarter):
            out_ref[k] = hold[first + k]


def project(own, near, here, mine, other, acts, grad):
    blocks, (rank, width) = acts.shape[0] // BLOCK, mine.shape[1:]
    quarter = -(-2 * blocks // SIDE)
    return pl.pallas_call(
        functools.partial(project_kernel, blocks),
        out_shape=(jax.ShapeDtypeStruct((blocks, rank, width), BF),)
        + (jax.ShapeDtypeStruct((quarter, rank, BLOCK), BF),) * SIDE,
        in_specs=[SMEM()] * 3 + [VMEM()] * 4,
        out_specs=(VMEM(),) * (1 + SIDE),
        scratch_shapes=[pltpu.VMEM((SIDE * quarter, rank, BLOCK), BF)],
        compiler_params=PARAMS,
        cost_estimate=pl.CostEstimate(flops=0, bytes_accessed=8 * 2**20, transcendentals=0),
        name="project_ranks",
    )(own, near, here, mine, other, acts, grad)


def contribute_kernel(blocks, here_ref, *refs):
    parts, (acts_ref, grad_ref, ranks_ref, a_ref, b_ref, hold) = refs[:SIDE], refs[SIDE:]
    quarter = parts[0].shape[0]
    for step, part in enumerate(parts):
        first = lax.rem(here_ref[0] + SIDE - step, SIDE) * quarter
        for k in range(quarter):
            hold[first + k] = part[k]
    for n in range(blocks):
        rows = pl.ds(n * BLOCK, BLOCK)
        ranks_ref[n] = hold[n]
        a_ref[n] = (
            SCALE * jnp.dot(hold[n], acts_ref[rows, :], preferred_element_type=F32)
        ).astype(BF)
        b_ref[n] = (
            SCALE * jnp.dot(hold[blocks + n], grad_ref[rows, :], preferred_element_type=F32)
        ).astype(BF)


def contribute(here, parts, acts, grad):
    blocks, width = acts.shape[0] // BLOCK, acts.shape[1]
    quarter, rank = parts[0].shape[:2]
    shape = jax.ShapeDtypeStruct((blocks, rank, width), BF)
    return pl.pallas_call(
        functools.partial(contribute_kernel, blocks),
        out_shape=(jax.ShapeDtypeStruct((blocks, rank, BLOCK), BF), shape, shape),
        in_specs=[SMEM()] + [VMEM()] * (2 + SIDE),
        out_specs=(VMEM(),) * 3,
        scratch_shapes=[pltpu.VMEM((SIDE * quarter, rank, BLOCK), BF)],
        compiler_params=PARAMS,
        cost_estimate=pl.CostEstimate(flops=0, bytes_accessed=8 * 2**20, transcendentals=0),
        name="factor_contributions",
    )(here, *parts, acts, grad)


def total_kernel(needs, place, used, *refs):
    a_refs, b_refs, (mine_ref, other_ref) = refs[:7], refs[7:14], refs[14:]

    def one(need, parts):
        value = None
        for source, part in enumerate(parts):
            at = need * 8 + source
            term = part[place[at]].astype(F32) * used[at].astype(F32)
            value = term if value is None else value + term
        return value

    @pl.loop(0, needs)
    def _(need):
        mine_ref[need] = one(need, a_refs)
        mine_ref[needs + need] = one(need, b_refs)
        other_ref[need] = one(needs + need, a_refs)
        other_ref[needs + need] = one(needs + need, b_refs)


def total(place, used, parts_a, parts_b, needs):
    shape = jax.ShapeDtypeStruct((2 * needs,) + parts_a[0].shape[1:], F32)
    return pl.pallas_call(
        functools.partial(total_kernel, needs),
        out_shape=(shape, shape),
        in_specs=[SMEM()] * 2 + [VMEM()] * 14,
        out_specs=(VMEM(),) * 2,
        compiler_params=PARAMS,
        cost_estimate=pl.CostEstimate(flops=0, bytes_accessed=16 * 2**20, transcendentals=0),
        name="gradient_totals",
    )(place, used, *parts_a, *parts_b)


def far_term(place, used, far_ref, need):
    at = need * 8 + 7
    return far_ref[place[at]].astype(F32) * used[at].astype(F32)


def share_kernel(needs, place, used, far_a, far_b, near_ref, out_ref):
    @pl.loop(0, needs)
    def _(need):
        for k, far in enumerate((far_a, far_b)):
            at = k * needs + need
            out_ref[at] = (
                near_ref[at] + far_term(place, used, far, needs + need)
            ).astype(BF)


def share(place, used, far_a, far_b, near):
    return pl.pallas_call(
        functools.partial(share_kernel, near.shape[0] // 2),
        out_shape=jax.ShapeDtypeStruct(near.shape, BF),
        in_specs=[SMEM()] * 2 + [VMEM()] * 3,
        out_specs=VMEM(),
        compiler_params=PARAMS,
        cost_estimate=pl.CostEstimate(flops=0, bytes_accessed=4 * 2**20, transcendentals=0),
        name="gradient_share",
    )(place, used, far_a, far_b, near)


def update_kernel(
    slots, rolls, place, used, own_ref, a_ref, b_ref, mine_roll, other_roll,
    far_a, far_b, mine_ref, other_ref, new_a, new_b, roll_a, roll_b,
):
    needs = slots + rolls

    def fresh(factor, at, far):
        gradient = (
            mine_ref[at]
            + far_term(place, used, far, at % needs)
            + other_ref[at].astype(F32)
        )
        return (factor.astype(F32) - LEARN_RATE * gradient).astype(BF)

    for n in range(slots):
        new_a[n] = fresh(a_ref[n], n, far_a)
        new_b[n] = fresh(b_ref[n], needs + n, far_b)
    for n in range(rolls):
        own = own_ref[n] == 1
        roll_a[n] = fresh(jnp.where(own, mine_roll[n], other_roll[n]), slots + n, far_a)
        roll_b[n] = fresh(
            jnp.where(own, mine_roll[rolls + n], other_roll[rolls + n]), needs + slots + n, far_b
        )


def update(place, used, own, factor_a, factor_b, mine_roll, other_roll, far_a, far_b, mine, other):
    slots, rank, width = factor_a.shape
    rolls = mine_roll.shape[0] // 2
    shape = lambda n: jax.ShapeDtypeStruct((n, rank, width), BF)
    return pl.pallas_call(
        functools.partial(update_kernel, slots, rolls),
        out_shape=(shape(slots), shape(slots), shape(rolls), shape(rolls)),
        in_specs=[SMEM()] * 3 + [VMEM()] * 8,
        out_specs=(VMEM(),) * 4,
        compiler_params=PARAMS,
        cost_estimate=pl.CostEstimate(flops=0, bytes_accessed=8 * 2**20, transcendentals=0),
        name="update_factors",
    )(place, used, own, factor_a, factor_b, mine_roll, other_roll, far_a, far_b, mine, other)


def product(grad, weight):
    return lax.dot_general(grad, weight, (((1,), (1,)), ((), ())), preferred_element_type=F32)


def products_kernel(grad_ref, weight_ref, out_ref, held, done, came, left):
    step, steps = pl.program_id(0), held.shape[0]
    tile, (slots, blocks, rows, width) = held.shape[1], done.shape
    half = rows // 2

    def arriving(at):
        return pltpu.make_async_copy(weight_ref.at[pl.ds(at * tile, tile)], held.at[at], came.at[at])

    def leaving(at, k, part):
        slot, here = lax.rem(at, slots), pl.ds(part * half, half)
        return pltpu.make_async_copy(
            done.at[slot, k, here], out_ref.at[at * blocks + k, here], left.at[slot, k, part]
        )

    @pl.when(step == 0)
    def _():
        for at in range(steps):
            arriving(at).start()

    arriving(step).wait()

    @pl.when(step >= slots)
    def _():
        for k in range(blocks):
            for part in range(2):
                leaving(step - slots, k, part).wait()

    for k in range(blocks):
        weight = held[step, k * width : (k + 1) * width, :]
        done[lax.rem(step, slots), k] = product(grad_ref[...], weight).astype(BF)
        for part in range(2):
            leaving(step, k, part).start()

    @pl.when(step == steps - 1)
    def _():
        for back in range(slots - 1, -1, -1):
            for k in range(blocks):
                for part in range(2):
                    leaving(step - back, k, part).wait()


def products(grad, weight, blocks):
    (rows, depth), columns = grad.shape, weight.shape[0]
    width, tile = columns // blocks, TILE
    steps, each = columns // tile, tile // width
    return pl.pallas_call(
        products_kernel,
        grid=(steps,),
        out_shape=jax.ShapeDtypeStruct((blocks, rows, width), BF),
        in_specs=[pl.BlockSpec((rows, depth), lambda j: (0, 0)), ANY()],
        out_specs=ANY(),
        scratch_shapes=[
            pltpu.VMEM((steps, tile, depth), BF),
            pltpu.VMEM((2, each, rows, width), BF),
            pltpu.SemaphoreType.DMA((steps,)),
            pltpu.SemaphoreType.DMA((2, each, 2)),
        ],
        compiler_params=pltpu.CompilerParams(vmem_limit_bytes=BASE_VMEM),
        cost_estimate=pl.CostEstimate(
            flops=2 * rows * depth * columns, bytes_accessed=24 * 2**20, transcendentals=0
        ),
        name="base_products",
    )(grad, weight)


def finish_kernel(blocks, ranks_ref, chosen_ref, base_ref, out_ref):
    for n in range(blocks):
        rows = pl.ds(n * BLOCK, BLOCK)
        term = lax.dot_general(
            ranks_ref[n], chosen_ref[n], (((0,), (0,)), ((), ())), preferred_element_type=F32
        )
        out_ref[rows, :] = (base_ref[0, rows, :].astype(F32) + SCALE * term).astype(BF)


def finish(ranks, chosen, base):
    blocks = chosen.shape[0]
    return pl.pallas_call(
        functools.partial(finish_kernel, blocks),
        out_shape=jax.ShapeDtypeStruct(base.shape[1:], BF),
        in_specs=[VMEM()] * 3,
        out_specs=VMEM(),
        compiler_params=PARAMS,
        cost_estimate=pl.CostEstimate(flops=0, bytes_accessed=4 * 2**20, transcendentals=0),
        name="input_gradient",
    )(ranks, chosen, base)


def per_device(
    input_acts, out_grad, base_weight, factor_a, factor_b, block_adapter, adapter_slot, rollout_map
):
    blocks = block_adapter.shape[0]
    slots = factor_a.shape[0]
    rolls = rollout_map.size
    groups = lax.axis_size("dp")
    chips = groups // CORES
    me = lax.axis_index("dp")
    chip, core = me // CORES, me % CORES

    wanted = slot_lookup(jnp.concatenate([block_adapter, rollout_map.reshape(-1)]), adapter_slot)
    other_wanted = core_swap(wanted)
    other = me ^ 1

    def places(slot_ids):
        owner = slot_ids // slots
        here = owner % CORES == core
        distance = (owner // CORES - chip + chips) % chips
        return jnp.where(here, distance * slots + slot_ids % slots, 0), here.astype(jnp.int32)

    mine_place, mine_own = places(wanted)
    other_place, other_own = places(other_wanted)

    def one_each(slot_ids, here):
        distance = (slot_ids // slots // CORES - chip + chips) % chips
        hit = (distance[None] == jnp.arange(chips, dtype=jnp.int32)[:, None]) & (here[None] == 1)
        return jnp.sum(jnp.where(hit, slot_ids[None] % slots, 0), axis=1)

    mine_within = one_each(wanted[:blocks], mine_own[:blocks])
    other_within = one_each(other_wanted[:blocks], other_own[:blocks])
    mine_near = (wanted[:blocks] // slots // CORES - chip + chips) % chips

    partial_value = products(out_grad, base_weight, lax.axis_size("tensor"))
    base = lax.psum_scatter(partial_value, "tensor", scatter_dimension=0, tiled=True)

    width = factor_a.shape[2]
    ids = jnp.pad(wanted[None].astype(BF), ((0, 15), (0, width - blocks - rolls)))
    parts_a, parts_b = ring_gather(
        factor_a.reshape(-1, width), jnp.concatenate([factor_b.reshape(-1, width), ids])
    )
    mine_sel, other_sel, mine_roll, other_roll, ring_ids = pick(
        mine_within, other_within,
        jnp.concatenate([mine_place[blocks:], other_place[blocks:]]),
        parts_a, parts_b, factor_a.shape[1],
    )
    got_sel = core_swap(other_sel)
    here = (lax.axis_index("tensor") % SIDE).reshape(1)
    chosen_a, *rank_parts = project(
        mine_own[:blocks], mine_near, here, mine_sel, got_sel, input_acts, out_grad
    )
    got_roll = core_swap(other_roll)
    quarter = rank_parts[0]
    for axis, terms in (("y", rank_parts), ("x", None)):
        terms = terms or [quarter] * SIDE
        came = [plane_hop(terms[step], step, axis) for step in range(1, SIDE)]
        quarter = sum(term.astype(F32) for term in [quarter, *came]).astype(BF)
    ranks, part_a, part_b = contribute(
        here,
        [quarter] + [plane_hop(quarter, step, "y") for step in range(1, SIDE)],
        input_acts, out_grad,
    )

    order = [0, 1, 2, 3, 5, 6, 7, 4]
    ring = ring_ids[:, 0, :blocks].astype(jnp.int32)
    ring = jnp.stack([ring[k] for k in order])
    own_slots = jnp.arange(slots, dtype=jnp.int32)
    need = jnp.concatenate(
        [me * slots + own_slots, wanted[blocks:], other * slots + own_slots, other_wanted[blocks:]]
    )
    match = (need[:, None, None] == ring[None]).astype(jnp.int32)
    used = jnp.sum(match, axis=2)
    at_block = jnp.sum(match * jnp.arange(blocks, dtype=jnp.int32)[None, None], axis=2)
    source, used = at_block.reshape(-1), used.reshape(-1)

    parts_a, parts_b = ring_gather(part_a, part_b)
    near = order[:7]
    mine_total, other_total = total(
        source, used, [parts_a[k] for k in near], [parts_b[k] for k in near], slots + rolls
    )
    got_total = core_swap(share(source, used, parts_a[4], parts_b[4], other_total))
    new_a, new_b, roll_a, roll_b = update(
        source, used, mine_own[blocks:], factor_a, factor_b, mine_roll, got_roll,
        parts_a[4], parts_b[4], mine_total, got_total,
    )
    return finish(ranks, chosen_a, base), new_a, new_b, roll_a, roll_b


def solution(mesh):
    return jax.shard_map(
        per_device,
        mesh=mesh,
        in_specs=(
            P("dp", "tensor"),
            P("dp", "tensor"),
            P(None, "tensor"),
            P("dp", None, "tensor"),
            P("dp", None, "tensor"),
            P("dp"),
            P(),
            P("dp", None),
        ),
        out_specs=(
            P("dp", "tensor"),
            P("dp", None, "tensor"),
            P("dp", None, "tensor"),
            P("dp", None, "tensor"),
            P("dp", None, "tensor"),
        ),
        check_vma=False,
    )
```
